256 devices in a mesh: leaf: 4 (over x), row: 8 (over z), col: 8 (over y, core).
Axes of the slice: x: 4, y: 4, z: 8, core: 2. Of those that a mesh axis runs over, the one named last changes fastest.
Arguments:
- child_rhs: bfloat16 [4, 2, 8, 256, 256], P('leaf', None, 'col'), may hold values from -6 to 6
- child_inv: bfloat16 [4, 2, 8, 256, 2, 8, 256], P('leaf', None, 'row', None, None, 'col')
- root_inv: bfloat16 [6, 8, 256, 6, 8, 256], P(None, 'row', None, None, 'col')
- coupling: bfloat16 [4, 2, 8, 256, 3, 8, 256], P('leaf', None, 'row', None, None, 'col'), may hold values from -0.09375 to 0.09375
- root_rhs: bfloat16 [6, 8, 256, 256], P(None, 'col'), may hold values from -6 to 6
- structure: int32 [4, 24], P('leaf'), may hold values from 0 to 47, as said below
Outputs:
- child_solution: float32 [4, 2, 8, 256, 256], P('leaf', None, 'col')
- root_solution: float32 [6, 8, 256, 256], P(None, 'col')
The draws below stay inside these ranges and needn't reach their ends.
Inputs may be any that keep to these rules, and one draw needn't show every extreme that they name: `structure`: within one child the 24 entries are distinct; different children may share root blocks.
All inputs are finite; a program needn't handle non-finite values.
Results may differ from the reference program's by a relative error of at most 0.008.
Values may be sent and summed in bfloat16 or wider, within the bound.
A program may use at most 64 MiB of HBM per device.

```python
import math
import jax
import jax.numpy as jnp

B = 256
NRHS = 256
RB_DEV = 6
CB_DEV = 2
KB_DEV = 3
NBR = 48
NBC = 16
KB = 24
RCOL = 6
CCOL = 2
CHILDREN = 4
N_ROW = 8
N_COL = 8


def triangle(key, width):
    first_key, second_key = jax.random.split(key)
    rows = jnp.arange(width)[:, None]
    cols = jnp.arange(width)[None, :]
    entries = jax.random.normal(first_key, (width, width), jnp.float32)
    diagonal = jax.random.uniform(second_key, (width,), jnp.float32, 0.6, 1.4)
    lower = jnp.where(rows > cols, entries * (1.5 / math.sqrt(width)), 0.0)
    return lower + jnp.where(rows == cols, diagonal[:, None], 0.0)


def draw_root_inv(key, part):
    full = triangle(jax.random.fold_in(key, 11), NBR * B)
    return full.reshape(RB_DEV, NBR // RB_DEV, B, RCOL, NBR // RCOL, B).astype(jnp.bfloat16)


def draw_child_inv(key, part):
    mats = [triangle(jax.random.fold_in(key, 100 + member), NBC * B) for member in range(CHILDREN)]
    full = jnp.stack(mats)
    return full.reshape(CHILDREN, CB_DEV, NBC // CB_DEV, B, CCOL, NBC // CCOL, B).astype(jnp.bfloat16)


def draw_structure(key, part):
    lists = [jax.random.permutation(jax.random.fold_in(key, 200 + member), NBR)[:KB] for member in range(CHILDREN)]
    stacked = jnp.stack(lists).astype(jnp.int32)
    leading = stacked[:, 0]
    order = jnp.arange(CHILDREN)
    shifts = jnp.where(order == 0, NBR - 1 - leading, jnp.where(order == 1, -leading, 0))
    return jnp.mod(stacked + shifts[:, None], NBR).astype(jnp.int32)


def level_of(key, dims, cuts, least, high):
    def one(axis_at, shards_of):
        draws = jax.random.uniform(jax.random.fold_in(jax.random.fold_in(key, 6), axis_at), (shards_of,), jnp.float32, least / len(cuts), high / len(cuts))
        return jnp.repeat(jnp.exp(draws), dims[axis_at] // shards_of).reshape((-1,) + (1,) * (len(dims) - axis_at - 1))

    factor_of = one(*cuts[0])
    for cut in cuts[1:]:
        factor_of = factor_of * one(*cut)
    return factor_of


def normal_values(rng, extent, scale, most, pieces=(), kind=jnp.bfloat16):
    values = scale * jax.random.normal(rng, extent, jnp.float32)
    if pieces:
        values = values * level_of(rng, extent, pieces, -0.22, 0.18)
    return jnp.clip(values, -most, most).astype(kind)


def setup_inputs(seed: int = 0) -> dict:
    key_of = jax.random.split(jax.random.key(seed), 7)
    return {
        "child_rhs": normal_values(key_of[0], (CHILDREN, CCOL, N_COL, B, NRHS), 1.0, 6.0, ((0, 4), (2, 8))),
        "child_inv": draw_child_inv(jax.random.fold_in(key_of[6], 71), 0),
        "root_inv": draw_root_inv(jax.random.fold_in(key_of[6], 71), 0),
        "coupling": normal_values(key_of[3], (CHILDREN, CB_DEV, N_ROW, B, KB_DEV, N_COL, B), (NBC * B) ** -0.5, 0.09375, ((0, 4), (2, 8), (5, 8))),
        "root_rhs": normal_values(key_of[4], (RCOL, N_COL, B, NRHS), 1.0, 6.0, ((1, 8),)),
        "structure": draw_structure(jax.random.fold_in(key_of[6], 71), 0),
    }


def reference(child_rhs, child_inv, root_inv, coupling, root_rhs, structure):
    root_width = NBR * B
    child_width = NBC * B
    root_mat = root_inv.reshape(root_width, root_width)
    update = jnp.zeros((NBR, B, NRHS), jnp.float32)
    forwards = []
    for member in range(CHILDREN):
        child_mat = child_inv[member].reshape(child_width, child_width)
        link_mat = coupling[member].reshape(child_width, KB * B)
        forward = jnp.dot(child_mat, child_rhs[member].reshape(child_width, NRHS), preferred_element_type=jnp.float32)
        lifted = jnp.dot(link_mat.T, forward.astype(jnp.bfloat16), preferred_element_type=jnp.float32)
        update = update.at[structure[member]].add(lifted.reshape(KB, B, NRHS))
        forwards.append(forward)
    residual = (root_rhs.reshape(root_width, NRHS).astype(jnp.float32) - update.reshape(root_width, NRHS)).astype(jnp.bfloat16)
    root_y = jnp.dot(root_mat, residual, preferred_element_type=jnp.float32).astype(jnp.bfloat16)
    root_x = jnp.dot(root_mat.T, root_y, preferred_element_type=jnp.float32)
    root_xb = root_x.astype(jnp.bfloat16).reshape(NBR, B, NRHS)
    solved = []
    for member in range(CHILDREN):
        child_mat = child_inv[member].reshape(child_width, child_width)
        link_mat = coupling[member].reshape(child_width, KB * B)
        needed = root_xb[structure[member]].reshape(KB * B, NRHS)
        carried = jnp.dot(link_mat, needed, preferred_element_type=jnp.float32)
        adjusted = (forwards[member] - carried).astype(jnp.bfloat16)
        solved.append(jnp.dot(child_mat.T, adjusted, preferred_element_type=jnp.float32))
    child_solution = jnp.stack(solved).reshape(CHILDREN, CCOL, N_COL, B, NRHS)
    root_solution = root_x.reshape(RCOL, N_COL, B, NRHS)
    return child_solution, root_solution
```

```python
import jax
import jax.numpy as jnp
from jax import lax
from jax.experimental import pallas as pl
from jax.experimental.pallas import tpu as pltpu
from jax.sharding import PartitionSpec as P

F32 = jnp.float32
BF16 = jnp.bfloat16
MESH = pl.DeviceIdType.MESH

(F_RS, F_AG, L_RS, L_X, L_C, U_AG, Y_RS, Y_AG, X_RS, X_C, N_X, N_AG, C_RS, A_AG, D_RS, D_AG,
 S_X, O_AG, O_X) = range(19)
TRANSFERS = 19


def swap_halves(v):
    flat = v.reshape(-1, 128)
    return pltpu.roll(flat, 64, 1).reshape(v.shape)


def left_half(shape):
    return lax.broadcasted_iota(jnp.int32, shape, len(shape) - 1) < 64


def pack_quarters(top, bottom):
    left = left_half(top.shape)
    return jnp.where(left, top, swap_halves(bottom)), jnp.where(left, swap_halves(top), bottom)


def kernel(
    child_h, rhs_h, link_h, root_h, root_rhs_h, structure_ref,
    child_out, root_out,
    child, rhs, link, root, root_rhs, child_t, link_t, root_t,
    f_send, f_recv, f_mine, f_all, l_send, l_recv, lx_send, lx_all, c_send, c_recv,
    u_all, spread, y_send, y_recv, y_all, x_send, x_recv, x_all, n_send, n_recv, n_all,
    c2_send, c2_recv, a_all, d_send, d_recv, d_all, o_all, o_recv,
    ids_v, ids, local_sem, send_sem, recv_sem,
):
    leaf, row, col = (lax.axis_index(a) for a in ("leaf", "row", "col"))
    place = {"leaf": leaf, "row": row, "col": col}
    size = {"leaf": 4, "row": 8, "col": 8}
    started = []

    def peer(axis, step):
        return lax.rem(place[axis] + step, size[axis])

    def start(number, axis, source, target):
        copies = []
        for step in range(1, size[axis]):
            there = peer(axis, step)
            copy = pltpu.make_async_remote_copy(
                src_ref=source(there), dst_ref=target(step),
                send_sem=send_sem.at[number, step], recv_sem=recv_sem.at[number, step],
                device_id={axis: there}, device_id_type=MESH,
            )
            copy.start()
            copies.append(copy)
        started.extend(copies)
        return copies

    def scatter(number, axis, parts, landing):
        return start(number, axis, lambda there: parts.at[there], lambda step: landing.at[step])

    def gather(number, axis, whole):
        mine = whole.at[place[axis]]
        return start(number, axis, lambda there: mine, lambda step: mine)

    def arrived(copies):
        for copy in copies:
            copy.wait_recv()

    def total(axis, parts, landing):
        value = parts[place[axis]].astype(F32)
        for step in range(1, size[axis]):
            value = value + landing[step].astype(F32)
        return value

    def dot(a, b):
        return jnp.dot(a, b, preferred_element_type=F32)

    loads = [
        pltpu.make_async_copy(src, dst, local_sem.at[n])
        for n, (src, dst) in enumerate(
            ((child_h, child), (rhs_h, rhs), (link_h, link), (root_rhs_h, root_rhs), (root_h, root))
        )
    ]
    for load in loads:
        load.start()

    barrier = pltpu.get_barrier_semaphore()
    for axis in ("leaf", "row", "col"):
        for step in range(1, size[axis]):
            pl.semaphore_signal(barrier, inc=1, device_id={axis: peer(axis, step)}, device_id_type=MESH)
    pl.semaphore_wait(barrier, 17)

    structure_copies = start(
        S_X, "leaf", lambda there: structure_ref, lambda step: ids_v.at[leaf]
    )
    ids_v[leaf] = structure_ref[...]

    loads[0].wait()
    loads[1].wait()
    for a in range(2):
        part = dot(child[a, 0], rhs[0]) + dot(child[a, 1], rhs[1])
        f_send[pl.ds(4 * a, 4)] = part.reshape(4, 64, 256).astype(BF16)
    copies = scatter(F_RS, "col", f_send, f_recv)
    loads[2].wait()
    for a in range(2):
        for m in range(3):
            link_t[m, a] = link[a, m].T
    arrived(copies)
    f_mine[...] = total("col", f_send, f_recv)
    f_all[col] = f_mine[...].astype(BF16)
    copies = gather(F_AG, "col", f_all)
    for a in range(2):
        for x in range(2):
            child_t[x, a] = child[a, x].T
    loads[3].wait()
    loads[4].wait()
    arrived(copies)

    for m in range(3):
        part = jnp.zeros((256, 256), F32)
        for a in range(2):
            part = part + dot(link_t[m, a], f_all[pl.ds(4 * a, 4)].reshape(256, 256))
        l_send[:, m] = part.reshape(8, 32, 256).astype(BF16)
    copies = scatter(L_RS, "row", l_send, l_recv)

    def turn(n, carry):
        a, x = n // 6, n % 6
        root_t[x * 6 + a] = root[a * 6 + x].T
        return carry

    lax.fori_loop(0, 36, turn, 0)
    arrived(structure_copies)
    to_scalars = pltpu.make_async_copy(ids_v, ids, local_sem.at[5])
    to_scalars.start()
    to_scalars.wait()
    arrived(copies)
    lifted = total("row", l_send, l_recv)
    for h in range(2):
        lanes = lifted[:, :, 128 * h : 128 * h + 128]
        for q, packed in enumerate(pack_quarters(lanes[:, :16], lanes[:, 16:])):
            lx_send[2 * h + q] = packed.astype(BF16)
    copies = start(L_X, "leaf", lambda there: lx_send.at[there], lambda step: lx_all.at[leaf])
    lx_all[leaf] = lx_send[leaf]
    arrived(copies)

    block = lax.broadcasted_iota(jnp.int32, (6, 16, 128), 0) * 8
    for target in range(8):
        value = jnp.zeros((6, 16, 128), F32)
        for child_at in range(4):
            for m in range(3):
                wanted = ids[child_at, 0, col + 8 * m] - target
                value = value + jnp.where(block == wanted, lx_all[child_at, m].astype(F32)[None], 0.0)
        c_send[target] = value.astype(BF16)
    copies = scatter(L_C, "col", c_send, c_recv)
    base = root_rhs[:, pl.ds(pl.multiple_of(row * 32, 32), 32), pl.ds(pl.multiple_of((leaf // 2) * 128, 128), 128)]
    base = base.astype(F32)
    first, second = pack_quarters(base[:, :16], base[:, 16:])
    base = jnp.where(leaf % 2 == 0, first, second)
    arrived(copies)
    update = total("col", c_send, c_recv)
    u_all[row] = (base - update).astype(BF16)
    copies = gather(U_AG, "row", u_all)
    left = left_half((8, 16, 128))
    keep_left = jnp.where(left, 1.0, 0.0).astype(BF16)
    keep_right = jnp.where(left, 0.0, 1.0).astype(BF16)

    def spread_out(whole):
        for a in range(6):
            spread[a, :, 0] = whole[:, a] * keep_left
            spread[a, :, 1] = whole[:, a] * keep_right

    def root_product(matrix, parts):
        for a in range(6):
            value = jnp.zeros((256, 128), F32)
            for x in range(6):
                value = value + dot(matrix[a * 6 + x], spread[x].reshape(256, 128))
            value = value + swap_halves(value)
            value = value.reshape(8, 2, 16, 128)
            parts[:, a] = jnp.where(left, value[:, 0], value[:, 1]).astype(BF16)

    arrived(copies)
    spread_out(u_all)
    root_product(root, y_send)
    copies = scatter(Y_RS, "col", y_send, y_recv)
    arrived(copies)
    y_all[col] = total("col", y_send, y_recv).astype(BF16)
    copies = gather(Y_AG, "col", y_all)
    arrived(copies)
    spread_out(y_all)
    root_product(root_t, x_send)
    copies = scatter(X_RS, "row", x_send, x_recv)
    arrived(copies)
    solved = total("row", x_send, x_recv).astype(BF16)
    x_all[col] = solved
    copies = gather(X_C, "col", x_all)
    o_all[row] = solved
    out_copies = gather(O_AG, "row", o_all)
    arrived(copies)

    for child_at in range(4):
        for m in range(3):
            r = ids[child_at, 0, col + 8 * m]
            n_send[child_at, m] = x_all[r & 7, r >> 3]
    copies = start(N_X, "leaf", lambda there: n_send.at[there], lambda step: n_recv.at[leaf])
    n_recv[leaf] = n_send[leaf]

    def unpack(even, odd):
        even, odd = even.astype(F32), odd.astype(F32)
        mask = left_half(even.shape)
        top = jnp.where(mask, even, swap_halves(odd))
        bottom = jnp.where(mask, swap_halves(even), odd)
        return top.astype(BF16), bottom.astype(BF16)

    arrived(copies)
    for h in range(2):
        top, bottom = unpack(n_recv[2 * h], n_recv[2 * h + 1])
        n_all[row, :, pl.ds(0, 16), pl.ds(128 * h, 128)] = top
        n_all[row, :, pl.ds(16, 16), pl.ds(128 * h, 128)] = bottom
    copies = gather(N_AG, "row", n_all)
    arrived(copies)

    for a in range(2):
        part = jnp.zeros((256, 256), F32)
        for m in range(3):
            part = part + dot(link[a, m], n_all[:, m].reshape(256, 256))
        c2_send[pl.ds(4 * a, 4)] = part.reshape(4, 64, 256).astype(BF16)
    copies = scatter(C_RS, "col", c2_send, c2_recv)
    arrived(out_copies)
    o_recv[leaf] = o_all[...]
    out_copies = start(O_X, "leaf", lambda there: o_all, lambda step: o_recv.at[leaf])
    arrived(copies)
    a_all[col] = (f_mine[...] - total("col", c2_send, c2_recv)).astype(BF16)
    copies = gather(A_AG, "col", a_all)
    arrived(copies)

    for x in range(2):
        part = jnp.zeros((256, 256), F32)
        for a in range(2):
            part = part + dot(child_t[x, a], a_all[pl.ds(4 * a, 4)].reshape(256, 256))
        d_send[pl.ds(4 * x, 4)] = part.reshape(4, 64, 256).astype(BF16)
    copies = scatter(D_RS, "row", d_send, d_recv)
    arrived(out_copies)
    for h in range(2):
        for r in range(8):
            top, bottom = unpack(o_recv[2 * h, r], o_recv[2 * h + 1, r])
            root_out[:, pl.ds(32 * r, 16), pl.ds(128 * h, 128)] = top
            root_out[:, pl.ds(32 * r + 16, 16), pl.ds(128 * h, 128)] = bottom
    arrived(copies)
    d_all[row] = total("row", d_send, d_recv).astype(BF16)
    copies = gather(D_AG, "row", d_all)
    arrived(copies)
    child_out[...] = d_all[...]
    for copy in started:
        copy.wait_send()


def on_device(child_rhs, child_inv, root_inv, coupling, root_rhs, structure):
    child = child_inv[0, :, 0, :, :, 0, :].transpose(0, 2, 1, 3)
    rhs = child_rhs[0, :, 0]
    link = coupling[0, :, 0, :, :, 0, :].transpose(0, 2, 1, 3)
    root = root_inv[:, 0, :, :, 0, :].transpose(0, 2, 1, 3).reshape(36, 256, 256)
    away = pl.BlockSpec(memory_space=pl.ANY)
    near = pl.BlockSpec(memory_space=pltpu.VMEM)
    packed = (6, 16, 128)
    shapes = [
        (2, 2, 256, 256), (2, 256, 256), (2, 3, 256, 256), (36, 256, 256), (6, 256, 256),
        (2, 2, 256, 256), (3, 2, 256, 256), (36, 256, 256),
        (8, 64, 256), (8, 64, 256), None, (8, 64, 256),
        (8, 3, 32, 256), (8, 3, 32, 256), (4, 3, 16, 128), (4, 3, 16, 128), (8,) + packed, (8,) + packed,
        (8,) + packed, (6, 8, 2, 16, 128),
        (8,) + packed, (8,) + packed, (8,) + packed,
        (8,) + packed, (8,) + packed, (8,) + packed,
        (4, 3, 16, 128), (4, 3, 16, 128), (8, 3, 32, 256),
        (8, 64, 256), (8, 64, 256), (8, 64, 256),
        (8, 64, 256), (8, 64, 256), (8, 64, 256),
        (8,) + packed, (4, 8) + packed,
    ]
    scratch = [
        pltpu.VMEM((64, 256), F32) if shape is None else pltpu.VMEM(shape, BF16) for shape in shapes
    ]
    scratch += [
        pltpu.VMEM((4, 1, 24), jnp.int32),
        pltpu.SMEM((4, 1, 24), jnp.int32),
        pltpu.SemaphoreType.DMA((6,)),
        pltpu.SemaphoreType.DMA((TRANSFERS, 8)),
        pltpu.SemaphoreType.DMA((TRANSFERS, 8)),
    ]
    child_x, root_x = pl.pallas_call(
        kernel,
        out_shape=(
            jax.ShapeDtypeStruct((8, 64, 256), BF16),
            jax.ShapeDtypeStruct((6, 256, 256), BF16),
        ),
        in_specs=[away] * 5 + [near],
        out_specs=(near, near),
        scratch_shapes=scratch,
        compiler_params=pltpu.CompilerParams(
            collective_id=0, has_side_effects=True, vmem_limit_bytes=40 * 1024 * 1024
        ),
        cost_estimate=pl.CostEstimate(flops=3_000_000_000, bytes_accessed=10_000_000, transcendentals=0),
        name="substitution",
    )(child, rhs, link, root, root_rhs[:, 0], structure)
    child_x = child_x.reshape(2, 256, 256).astype(F32)
    return child_x[None, :, None], root_x.astype(F32)[:, None]


def solution(mesh):
    placed = (
        P("leaf", None, "col", None, None),
        P("leaf", None, "row", None, None, "col", None),
        P(None, "row", None, None, "col", None),
        P("leaf", None, "row", None, None, "col", None),
        P(None, "col", None, None),
        P("leaf", None),
    )
    return jax.shard_map(
        on_device,
        mesh=mesh,
        in_specs=placed,
        out_specs=(P("leaf", None, "col", None, None), P(None, "col", None, None)),
        check_vma=False,
    )
```

```python
import jax
import jax.numpy as jnp
from jax import lax
from jax.experimental import pallas as pl
from jax.experimental.pallas import tpu as pltpu
from jax.sharding import PartitionSpec as P

F32 = jnp.float32
BF16 = jnp.bfloat16
MESH = pl.DeviceIdType.MESH

F_RS, F_AG, L_RS, N_AG, C_RS, A_AG, D_RS, D_AG = range(0, 16, 2)
L_X, L_C, U_AG, Y_RS, Y_AG, X_RS, X_C, N_X, S_X, O_AG, O_X = range(16, 27)
TRANSFERS = 27
HALVES = (0, 1)


def swap_halves(v):
    flat = v.reshape(-1, 128)
    return pltpu.roll(flat, 64, 1).reshape(v.shape)


def left_half(shape):
    return lax.broadcasted_iota(jnp.int32, shape, len(shape) - 1) < 64


def pack_quarters(top, bottom):
    left = left_half(top.shape)
    return jnp.where(left, top, swap_halves(bottom)), jnp.where(left, swap_halves(top), bottom)


def kernel(
    child_h, rhs_h, link_h, root_h, root_rhs_h, structure_ref,
    child_out_h, root_out_h,
    child, rhs, link, root, root_rhs, child_t, link_t, root_t,
    f_send, f_recv, f_mine, f_all, l_send, l_recv, lx_send, lx_all, c_send, c_recv,
    u_all, spread, y_send, y_recv, y_all, x_send, x_recv, x_all, n_send, n_recv, n_all,
    c2_send, c2_recv, a_all, d_send, d_recv, d_all, o_all, o_recv, child_out, root_out,
    ids_v, ids, local_sem, send_sem, recv_sem,
):
    leaf, row, col = (lax.axis_index(a) for a in ("leaf", "row", "col"))
    place = {"leaf": leaf, "row": row, "col": col}
    size = {"leaf": 4, "row": 8, "col": 8}
    started = []

    def peer(axis, step):
        return lax.rem(place[axis] + step, size[axis])

    def start(number, axis, source, target):
        copies = []
        for step in range(1, size[axis]):
            there = peer(axis, step)
            copy = pltpu.make_async_remote_copy(
                src_ref=source(there), dst_ref=target(step),
                send_sem=send_sem.at[number, step], recv_sem=recv_sem.at[number, step],
                device_id={axis: there}, device_id_type=MESH,
            )
            copy.start()
            copies.append(copy)
        started.extend(copies)
        return copies

    def scatter(number, axis, parts, landing):
        return start(number, axis, lambda there: parts.at[there], lambda step: landing.at[step])

    def gather(number, axis, whole):
        mine = whole.at[place[axis]]
        return start(number, axis, lambda there: mine, lambda step: mine)

    def arrived(copies):
        for copy in copies:
            copy.wait_recv()

    def total(axis, parts, landing):
        value = parts[place[axis]].astype(F32)
        for step in range(1, size[axis]):
            value = value + landing[step].astype(F32)
        return value

    def dot(a, b):
        return jnp.dot(a, b, preferred_element_type=F32)

    loads = [
        pltpu.make_async_copy(src, dst, local_sem.at[n])
        for n, (src, dst) in enumerate(
            ((child_h, child), (rhs_h, rhs), (link_h, link), (root_rhs_h, root_rhs), (root_h, root))
        )
    ]
    for load in loads:
        load.start()

    barrier = pltpu.get_barrier_semaphore()
    for axis in ("leaf", "row", "col"):
        for step in range(1, size[axis]):
            pl.semaphore_signal(barrier, inc=1, device_id={axis: peer(axis, step)}, device_id_type=MESH)
    pl.semaphore_wait(barrier, 17)

    structure_copies = start(
        S_X, "leaf", lambda there: structure_ref, lambda step: ids_v.at[leaf]
    )
    ids_v[leaf] = structure_ref[...]

    loads[0].wait()
    loads[1].wait()
    flight = {}
    for h in HALVES:
        lanes = slice(128 * h, 128 * h + 128)
        for a in range(2):
            part = dot(child[a, 0], rhs[0, :, lanes]) + dot(child[a, 1], rhs[1, :, lanes])
            f_send[h, pl.ds(4 * a, 4)] = part.reshape(4, 64, 128).astype(BF16)
        flight[h] = scatter(F_RS + h, "col", f_send.at[h], f_recv.at[h])
    loads[2].wait()
    for a in range(2):
        for m in range(3):
            link_t[m, a] = link[a, m].T
    for h in HALVES:
        arrived(flight[h])
        f_mine[h] = total("col", f_send.at[h], f_recv.at[h])
        f_all[h, col] = f_mine[h].astype(BF16)
        flight[h] = gather(F_AG + h, "col", f_all.at[h])
    for a in range(2):
        for x in range(2):
            child_t[x, a] = child[a, x].T

    for h in HALVES:
        arrived(flight[h])
        for m in range(3):
            part = jnp.zeros((256, 128), F32)
            for a in range(2):
                part = part + dot(link_t[m, a], f_all[h, pl.ds(4 * a, 4)].reshape(256, 128))
            l_send[h, :, m] = part.reshape(8, 32, 128).astype(BF16)
        flight[h] = scatter(L_RS + h, "row", l_send.at[h], l_recv.at[h])
    loads[3].wait()
    loads[4].wait()

    def turn(n, carry):
        a, x = n // 6, n % 6
        root_t[x * 6 + a] = root[a * 6 + x].T
        return carry

    lax.fori_loop(0, 36, turn, 0)
    arrived(structure_copies)
    to_scalars = pltpu.make_async_copy(ids_v, ids, local_sem.at[5])
    to_scalars.start()
    to_scalars.wait()
    for h in HALVES:
        arrived(flight[h])
        lifted = total("row", l_send.at[h], l_recv.at[h])
        for q, packed in enumerate(pack_quarters(lifted[:, :16], lifted[:, 16:])):
            lx_send[2 * h + q] = packed.astype(BF16)
    copies = start(L_X, "leaf", lambda there: lx_send.at[there], lambda step: lx_all.at[leaf])
    lx_all[leaf] = lx_send[leaf]
    arrived(copies)

    block = lax.broadcasted_iota(jnp.int32, (6, 16, 128), 0) * 8
    for target in range(8):
        value = jnp.zeros((6, 16, 128), F32)
        for child_at in range(4):
            for m in range(3):
                wanted = ids[child_at, 0, col + 8 * m] - target
                value = value + jnp.where(block == wanted, lx_all[child_at, m].astype(F32)[None], 0.0)
        c_send[target] = value.astype(BF16)
    copies = scatter(L_C, "col", c_send, c_recv)
    base = root_rhs[:, pl.ds(pl.multiple_of(row * 32, 32), 32), pl.ds(pl.multiple_of((leaf // 2) * 128, 128), 128)]
    base = base.astype(F32)
    first, second = pack_quarters(base[:, :16], base[:, 16:])
    base = jnp.where(leaf % 2 == 0, first, second)
    arrived(copies)
    update = total("col", c_send, c_recv)
    u_all[row] = (base - update).astype(BF16)
    copies = gather(U_AG, "row", u_all)
    left = left_half((8, 16, 128))
    keep_left = jnp.where(left, 1.0, 0.0).astype(BF16)
    keep_right = jnp.where(left, 0.0, 1.0).astype(BF16)

    def spread_out(whole):
        for a in range(6):
            spread[a, :, 0] = whole[:, a] * keep_left
            spread[a, :, 1] = whole[:, a] * keep_right

    def root_product(matrix, parts):
        for a in range(6):
            value = jnp.zeros((256, 128), F32)
            for x in range(6):
                value = value + dot(matrix[a * 6 + x], spread[x].reshape(256, 128))
            value = value + swap_halves(value)
            value = value.reshape(8, 2, 16, 128)
            parts[:, a] = jnp.where(left, value[:, 0], value[:, 1]).astype(BF16)

    arrived(copies)
    spread_out(u_all)
    root_product(root, y_send)
    copies = scatter(Y_RS, "col", y_send, y_recv)
    arrived(copies)
    y_all[col] = total("col", y_send, y_recv).astype(BF16)
    copies = gather(Y_AG, "col", y_all)
    arrived(copies)
    spread_out(y_all)
    root_product(root_t, x_send)
    copies = scatter(X_RS, "row", x_send, x_recv)
    arrived(copies)
    solved = total("row", x_send, x_recv).astype(BF16)
    x_all[col] = solved
    copies = gather(X_C, "col", x_all)
    o_all[row] = solved
    out_copies = gather(O_AG, "row", o_all)
    arrived(copies)

    for child_at in range(4):
        for m in range(3):
            r = ids[child_at, 0, col + 8 * m]
            n_send[child_at, m] = x_all[r & 7, r >> 3]
    copies = start(N_X, "leaf", lambda there: n_send.at[there], lambda step: n_recv.at[leaf])
    n_recv[leaf] = n_send[leaf]

    def unpack(even, odd):
        even, odd = even.astype(F32), odd.astype(F32)
        mask = left_half(even.shape)
        top = jnp.where(mask, even, swap_halves(odd))
        bottom = jnp.where(mask, swap_halves(even), odd)
        return top.astype(BF16), bottom.astype(BF16)

    arrived(copies)
    for h in HALVES:
        top, bottom = unpack(n_recv[2 * h], n_recv[2 * h + 1])
        n_all[h, row, :, pl.ds(0, 16)] = top
        n_all[h, row, :, pl.ds(16, 16)] = bottom
        flight[h] = gather(N_AG + h, "row", n_all.at[h])

    for h in HALVES:
        arrived(flight[h])
        for a in range(2):
            part = jnp.zeros((256, 128), F32)
            for m in range(3):
                part = part + dot(link[a, m], n_all[h, :, m].reshape(256, 128))
            c2_send[h, pl.ds(4 * a, 4)] = part.reshape(4, 64, 128).astype(BF16)
        flight[h] = scatter(C_RS + h, "col", c2_send.at[h], c2_recv.at[h])
    arrived(out_copies)
    o_recv[leaf] = o_all[...]
    out_copies = start(O_X, "leaf", lambda there: o_all, lambda step: o_recv.at[leaf])
    for h in HALVES:
        arrived(flight[h])
        a_all[h, col] = (f_mine[h] - total("col", c2_send.at[h], c2_recv.at[h])).astype(BF16)
        flight[h] = gather(A_AG + h, "col", a_all.at[h])

    for h in HALVES:
        arrived(flight[h])
        for x in range(2):
            part = jnp.zeros((256, 128), F32)
            for a in range(2):
                part = part + dot(child_t[x, a], a_all[h, pl.ds(4 * a, 4)].reshape(256, 128))
            d_send[h, pl.ds(4 * x, 4)] = part.reshape(4, 64, 128).astype(BF16)
        flight[h] = scatter(D_RS + h, "row", d_send.at[h], d_recv.at[h])
    for h in HALVES:
        arrived(flight[h])
        d_all[h, row] = total("row", d_send.at[h], d_recv.at[h]).astype(BF16)
        flight[h] = gather(D_AG + h, "row", d_all.at[h])
    arrived(out_copies)
    for h in HALVES:
        for r in range(8):
            top, bottom = unpack(o_recv[2 * h, r], o_recv[2 * h + 1, r])
            root_out[:, pl.ds(32 * r, 16), pl.ds(128 * h, 128)] = top
            root_out[:, pl.ds(32 * r + 16, 16), pl.ds(128 * h, 128)] = bottom
    root_store = pltpu.make_async_copy(root_out, root_out_h, local_sem.at[6])
    root_store.start()
    for h in HALVES:
        arrived(flight[h])
        child_out[:, :, pl.ds(128 * h, 128)] = d_all[h]
    child_store = pltpu.make_async_copy(child_out, child_out_h, local_sem.at[7])
    child_store.start()
    child_store.wait()
    root_store.wait()
    for copy in started:
        copy.wait_send()


def on_device(child_rhs, child_inv, root_inv, coupling, root_rhs, structure):
    child = child_inv[0, :, 0, :, :, 0, :].transpose(0, 2, 1, 3)
    rhs = child_rhs[0, :, 0]
    link = coupling[0, :, 0, :, :, 0, :].transpose(0, 2, 1, 3)
    root = root_inv[:, 0, :, :, 0, :].transpose(0, 2, 1, 3).reshape(36, 256, 256)
    away = pl.BlockSpec(memory_space=pltpu.HBM)
    near = pl.BlockSpec(memory_space=pltpu.VMEM)
    packed = (6, 16, 128)
    half = (2, 8, 64, 128)
    shapes = [
        (2, 2, 256, 256), (2, 256, 256), (2, 3, 256, 256), (36, 256, 256), (6, 256, 256),
        (2, 2, 256, 256), (3, 2, 256, 256), (36, 256, 256),
        half, half, None, half,
        (2, 8, 3, 32, 128), (2, 8, 3, 32, 128), (4, 3, 16, 128), (4, 3, 16, 128), (8,) + packed, (8,) + packed,
        (8,) + packed, (6, 8, 2, 16, 128),
        (8,) + packed, (8,) + packed, (8,) + packed,
        (8,) + packed, (8,) + packed, (8,) + packed,
        (4, 3, 16, 128), (4, 3, 16, 128), (2, 8, 3, 32, 128),
        half, half, half,
        half, half, half,
        (8,) + packed, (4, 8) + packed, (8, 64, 256), (6, 256, 256),
    ]
    scratch = [
        pltpu.VMEM((2, 64, 128), F32) if shape is None else pltpu.VMEM(shape, BF16) for shape in shapes
    ]
    scratch += [
        pltpu.VMEM((4, 1, 24), jnp.int32),
        pltpu.SMEM((4, 1, 24), jnp.int32),
        pltpu.SemaphoreType.DMA((8,)),
        pltpu.SemaphoreType.DMA((TRANSFERS, 8)),
        pltpu.SemaphoreType.DMA((TRANSFERS, 8)),
    ]
    child_x, root_x = pl.pallas_call(
        kernel,
        out_shape=(
            jax.ShapeDtypeStruct((8, 64, 256), BF16),
            jax.ShapeDtypeStruct((6, 256, 256), BF16),
        ),
        in_specs=[away] * 5 + [near],
        out_specs=(away, away),
        scratch_shapes=scratch,
        compiler_params=pltpu.CompilerParams(
            collective_id=0, has_side_effects=True, vmem_limit_bytes=60 * 1024 * 1024
        ),
        cost_estimate=pl.CostEstimate(flops=3_000_000_000, bytes_accessed=10_000_000, transcendentals=0),
        name="substitution",
    )(child, rhs, link, root, root_rhs[:, 0], structure)
    child_x = child_x.reshape(2, 256, 256).astype(F32)
    return child_x[None, :, None], root_x.astype(F32)[:, None]


def solution(mesh):
    placed = (
        P("leaf", None, "col", None, None),
        P("leaf", None, "row", None, None, "col", None),
        P(None, "row", None, None, "col", None),
        P("leaf", None, "row", None, None, "col", None),
        P(None, "col", None, None),
        P("leaf", None),
    )
    return jax.shard_map(
        on_device,
        mesh=mesh,
        in_specs=placed,
        out_specs=(P("leaf", None, "col", None, None), P(None, "col", None, None)),
        check_vma=False,
    )
```

```python
import jax
import jax.numpy as jnp
from jax import lax
from jax.experimental import pallas as pl
from jax.experimental.pallas import tpu as pltpu
from jax.sharding import PartitionSpec as P

F32 = jnp.float32
BF16 = jnp.bfloat16
MESH = pl.DeviceIdType.MESH

N_XZ, C_RS, A_AG, D_RS, D_AG = range(0, 10, 2)
F_RS, F_AG, L_XZ, L_C, U_AG, Y_RS, Y_AG, X_RS, X_C, S_X, O_AG, O_X = range(10, 22)
TRANSFERS = 22
HALVES = (0, 1)
FAR_FIRST = (4, 3, 5, 2, 6, 1, 7)


def swap_halves(v):
    flat = v.reshape(-1, 128)
    return pltpu.roll(flat, 64, 1).reshape(v.shape)


def left_half(shape):
    return lax.broadcasted_iota(jnp.int32, shape, len(shape) - 1) < 64


def pack_quarters(top, bottom):
    left = left_half(top.shape)
    return jnp.where(left, top, swap_halves(bottom)), jnp.where(left, swap_halves(top), bottom)


def kernel(
    child_h, rhs_h, link_h, root_h, root_rhs_h, structure_ref,
    child_out_h, root_out_h,
    child, rhs, link, root, root_rhs, child_t, link_t, root_t,
    f_send, f_recv, f_mine, f_all, l_send, l_recv, lx_all, c_send, c_recv,
    u_all, spread, y_send, y_recv, y_all, x_send, x_recv, x_all, n_send, n_recv, n_all,
    c2_send, c2_recv, a_all, d_send, d_recv, d_all, o_all, o_recv, child_out, root_out,
    ids_v, ids, local_sem, send_sem, recv_sem,
):
    leaf, row, col = (lax.axis_index(a) for a in ("leaf", "row", "col"))
    place = {"leaf": leaf, "row": row, "col": col}
    size = {"leaf": 4, "row": 8, "col": 8}
    sends = []

    def peer(axis, step):
        return lax.rem(place[axis] + step, size[axis])

    def copy(number, arrival, source, target, device):
        return pltpu.make_async_remote_copy(
            src_ref=source, dst_ref=target,
            send_sem=send_sem.at[number], recv_sem=recv_sem.at[arrival],
            device_id=device, device_id_type=MESH,
        )

    def start(number, axis, source, target, whole):
        for step in FAR_FIRST if size[axis] == 8 else (2, 1, 3):
            there = peer(axis, step)
            copy(number, number, source(there), target(step), {axis: there}).start()
        pending = copy(number, number, whole, whole, {axis: peer(axis, 1)})
        sends.append(pending)
        return pending

    def scatter(number, axis, parts, landing):
        return start(
            number, axis, lambda there: parts.at[there], lambda step: landing.at[step], parts.at[pl.ds(0, size[axis] - 1)]
        )

    def gather(number, axis, whole):
        mine = whole.at[place[axis]]
        return start(number, axis, lambda there: mine, lambda step: mine, whole.at[pl.ds(0, size[axis] - 1)])

    def arrived(pending):
        pending.wait_recv()

    def total(axis, parts, landing):
        value = parts[place[axis]].astype(F32)
        for step in range(1, size[axis]):
            value = value + landing[step].astype(F32)
        return value

    def dot(a, b):
        return jnp.dot(a, b, preferred_element_type=F32)

    loads = [
        pltpu.make_async_copy(src, dst, local_sem.at[n])
        for n, (src, dst) in enumerate(
            ((child_h, child), (rhs_h, rhs), (link_h, link), (root_rhs_h, root_rhs), (root_h, root))
        )
    ]
    loads[0].start()
    loads[1].start()
    barrier = pltpu.get_barrier_semaphore()
    for step in range(1, 8):
        pl.semaphore_signal(barrier, inc=1, device_id={"col": peer("col", step)}, device_id_type=MESH)
    for step in range(1, 32):
        there = {"leaf": peer("leaf", step // 8), "row": peer("row", step % 8)}
        pl.semaphore_signal(barrier, inc=1, device_id=there, device_id_type=MESH)
    ids_v[leaf] = structure_ref[...]

    loads[0].wait()
    loads[1].wait()
    for a in range(2):
        part = dot(child[a, 0], rhs[0]) + dot(child[a, 1], rhs[1])
        f_send[pl.ds(4 * a, 4)] = part.reshape(4, 64, 256).astype(BF16)
    pl.semaphore_wait(barrier, 38)
    pending = scatter(F_RS, "col", f_send, f_recv)
    for load in loads[2:]:
        load.start()
    structure_pending = start(
        S_X, "leaf", lambda there: structure_ref, lambda step: ids_v.at[leaf], ids_v.at[pl.ds(0, 3)]
    )
    loads[2].wait()
    for a in range(2):
        for m in range(3):
            link_t[m, a] = link[a, m].T
    arrived(pending)
    f_mine[...] = total("col", f_send, f_recv)
    f_all[col] = f_mine[...].astype(BF16)
    pending = gather(F_AG, "col", f_all)
    for a in range(2):
        for x in range(2):
            child_t[x, a] = child[a, x].T
    arrived(pending)

    for h in HALVES:
        for m in range(3):
            part = jnp.zeros((256, 128), F32)
            for a in range(2):
                part = part + dot(link_t[m, a], f_all[pl.ds(4 * a, 4), :, pl.ds(128 * h, 128)].reshape(256, 128))
            part = part.reshape(8, 2, 16, 128)
            for q, packed in enumerate(pack_quarters(part[:, 0], part[:, 1])):
                l_send[2 * h + q, :, m] = packed.astype(BF16)
        for step in FAR_FIRST:
            for there in (2 * h, 2 * h + 1):
                at = peer("row", step)
                copy(L_XZ, L_XZ, l_send.at[there, at], l_recv.at[leaf * 8 + step], {"leaf": there, "row": at}).start()
    for step in (2, 1, 3):
        there = peer("leaf", step)
        copy(L_XZ, L_XZ, l_send.at[there, row], l_recv.at[leaf * 8], {"leaf": there}).start()
    pltpu.make_async_copy(l_send.at[leaf, row], l_recv.at[leaf * 8], recv_sem.at[L_XZ]).start()
    pending = copy(L_XZ, L_XZ, l_recv.at[pl.ds(0, 31)], l_recv, {"row": peer("row", 1)})
    sends.append(pending)
    loads[3].wait()
    loads[4].wait()

    def turn(n, carry):
        a, x = n // 6, n % 6
        root_t[x * 6 + a] = root[a * 6 + x].T
        return carry

    lax.fori_loop(0, 36, turn, 0)
    arrived(structure_pending)
    to_scalars = pltpu.make_async_copy(ids_v, ids, local_sem.at[5])
    to_scalars.start()
    to_scalars.wait()
    arrived(pending)
    for child_at in range(4):
        value = l_recv[child_at * 8].astype(F32)
        for step in range(1, 8):
            value = value + l_recv[child_at * 8 + step].astype(F32)
        lx_all[child_at] = value

    block = lax.broadcasted_iota(jnp.int32, (6, 16, 128), 0) * 8
    for target in range(8):
        value = jnp.zeros((6, 16, 128), F32)
        for child_at in range(4):
            for m in range(3):
                wanted = ids[child_at, 0, col + 8 * m] - target
                value = value + jnp.where(block == wanted, lx_all[child_at, m][None], 0.0)
        c_send[target] = value.astype(BF16)
    pending = scatter(L_C, "col", c_send, c_recv)
    base = root_rhs[:, pl.ds(pl.multiple_of(row * 32, 32), 32), pl.ds(pl.multiple_of((leaf // 2) * 128, 128), 128)]
    base = base.astype(F32)
    first, second = pack_quarters(base[:, :16], base[:, 16:])
    base = jnp.where(leaf % 2 == 0, first, second)
    arrived(pending)
    u_all[row] = (base - total("col", c_send, c_recv)).astype(BF16)
    pending = gather(U_AG, "row", u_all)
    left = left_half((8, 16, 128))
    keep_left = jnp.where(left, 1.0, 0.0).astype(BF16)
    keep_right = jnp.where(left, 0.0, 1.0).astype(BF16)

    def spread_out(whole):
        for a in range(6):
            spread[a, :, 0] = whole[:, a] * keep_left
            spread[a, :, 1] = whole[:, a] * keep_right

    def root_product(matrix, parts):
        for a in range(6):
            value = jnp.zeros((256, 128), F32)
            for x in range(6):
                value = value + dot(matrix[a * 6 + x], spread[x].reshape(256, 128))
            value = value + swap_halves(value)
            value = value.reshape(8, 2, 16, 128)
            parts[:, a] = jnp.where(left, value[:, 0], value[:, 1]).astype(BF16)

    arrived(pending)
    spread_out(u_all)
    root_product(root, y_send)
    pending = scatter(Y_RS, "col", y_send, y_recv)
    arrived(pending)
    y_all[col] = total("col", y_send, y_recv).astype(BF16)
    pending = gather(Y_AG, "col", y_all)
    arrived(pending)
    spread_out(y_all)
    root_product(root_t, x_send)
    pending = scatter(X_RS, "row", x_send, x_recv)
    arrived(pending)
    solved = total("row", x_send, x_recv).astype(BF16)
    x_all[col] = solved
    pending = gather(X_C, "col", x_all)
    o_all[row] = solved
    arrived(pending)

    for child_at in range(4):
        for m in range(3):
            r = ids[child_at, 0, col + 8 * m]
            n_send[child_at, m] = x_all[r & 7, r >> 3]
    half_at = N_XZ + leaf // 2
    for step in FAR_FIRST + (0,):
        for leaf_step in (0, 1, 2, 3) if step else (1, 2, 3):
            there, at = peer("leaf", leaf_step), peer("row", step)
            copy(N_XZ, half_at, n_send.at[there], n_recv.at[leaf, row], {"leaf": there, "row": at}).start()
    pltpu.make_async_copy(n_send.at[leaf], n_recv.at[leaf, row], recv_sem.at[half_at]).start()
    sends.append(copy(N_XZ, N_XZ, l_recv.at[pl.ds(0, 31)], l_recv, {"row": peer("row", 1)}))
    out_pending = gather(O_AG, "row", o_all)

    def unpack(even, odd):
        even, odd = even.astype(F32), odd.astype(F32)
        mask = left_half(even.shape)
        top = jnp.where(mask, even, swap_halves(odd))
        bottom = jnp.where(mask, swap_halves(even), odd)
        return top.astype(BF16), bottom.astype(BF16)

    flight = {}
    for h in HALVES:
        pieces = n_recv.at[pl.ds(2 * h, 2)]
        arrived(copy(N_XZ, N_XZ + h, pieces, pieces, {"row": peer("row", 1)}))
        for m in range(3):
            n_all[m, :, 0], n_all[m, :, 1] = unpack(n_recv[2 * h, :, m], n_recv[2 * h + 1, :, m])
        for a in range(2):
            part = jnp.zeros((256, 128), F32)
            for m in range(3):
                part = part + dot(link[a, m], n_all[m].reshape(256, 128))
            c2_send[h, pl.ds(4 * a, 4)] = part.reshape(4, 64, 128).astype(BF16)
        flight[h] = scatter(C_RS + h, "col", c2_send.at[h], c2_recv.at[h])
    for h in HALVES:
        arrived(flight[h])
        carried = total("col", c2_send.at[h], c2_recv.at[h])
        a_all[h, col] = (f_mine[:, pl.ds(128 * h, 128)] - carried).astype(BF16)
        flight[h] = gather(A_AG + h, "col", a_all.at[h])
    arrived(out_pending)
    o_recv[leaf] = o_all[...]
    out_pending = start(O_X, "leaf", lambda there: o_all, lambda step: o_recv.at[leaf], o_recv.at[pl.ds(0, 3)])

    for h in HALVES:
        arrived(flight[h])
        for x in range(2):
            part = jnp.zeros((256, 128), F32)
            for a in range(2):
                part = part + dot(child_t[x, a], a_all[h, pl.ds(4 * a, 4)].reshape(256, 128))
            d_send[h, pl.ds(4 * x, 4)] = part.reshape(4, 64, 128).astype(BF16)
        flight[h] = scatter(D_RS + h, "row", d_send.at[h], d_recv.at[h])
    for h in HALVES:
        arrived(flight[h])
        d_all[h, row] = total("row", d_send.at[h], d_recv.at[h]).astype(BF16)
        flight[h] = gather(D_AG + h, "row", d_all.at[h])
    arrived(out_pending)
    for h in HALVES:
        for r in range(8):
            top, bottom = unpack(o_recv[2 * h, r], o_recv[2 * h + 1, r])
            root_out[:, pl.ds(32 * r, 16), pl.ds(128 * h, 128)] = top
            root_out[:, pl.ds(32 * r + 16, 16), pl.ds(128 * h, 128)] = bottom
    root_store = pltpu.make_async_copy(root_out, root_out_h, local_sem.at[6])
    root_store.start()
    for h in HALVES:
        arrived(flight[h])
        child_out[:, :, pl.ds(128 * h, 128)] = d_all[h]
    child_store = pltpu.make_async_copy(child_out, child_out_h, local_sem.at[7])
    child_store.start()
    child_store.wait()
    root_store.wait()
    for pending in sends:
        pending.wait_send()


def on_device(child_rhs, child_inv, root_inv, coupling, root_rhs, structure):
    child = child_inv[0, :, 0, :, :, 0, :].transpose(0, 2, 1, 3)
    rhs = child_rhs[0, :, 0]
    link = coupling[0, :, 0, :, :, 0, :].transpose(0, 2, 1, 3)
    root = root_inv[:, 0, :, :, 0, :].transpose(0, 2, 1, 3).reshape(36, 256, 256)
    away = pl.BlockSpec(memory_space=pltpu.HBM)
    near = pl.BlockSpec(memory_space=pltpu.VMEM)
    packed = (6, 16, 128)
    half = (2, 8, 64, 128)
    shapes = [
        (2, 2, 256, 256), (2, 256, 256), (2, 3, 256, 256), (36, 256, 256), (6, 256, 256),
        (2, 2, 256, 256), (3, 2, 256, 256), (36, 256, 256),
        (8, 64, 256), (8, 64, 256), None, (8, 64, 256),
        (4, 8, 3, 16, 128), (32, 3, 16, 128), None, (8,) + packed, (8,) + packed,
        (8,) + packed, (6, 8, 2, 16, 128),
        (8,) + packed, (8,) + packed, (8,) + packed,
        (8,) + packed, (8,) + packed, (8,) + packed,
        (4, 3, 16, 128), (4, 8, 3, 16, 128), (3, 8, 2, 16, 128),
        half, half, half,
        half, half, half,
        (8,) + packed, (4, 8) + packed, (8, 64, 256), (6, 256, 256),
    ]
    wide = iter([(64, 256), (4, 3, 16, 128)])
    scratch = [
        pltpu.VMEM(next(wide), F32) if shape is None else pltpu.VMEM(shape, BF16) for shape in shapes
    ]
    scratch += [
        pltpu.VMEM((4, 1, 24), jnp.int32),
        pltpu.SMEM((4, 1, 24), jnp.int32),
        pltpu.SemaphoreType.DMA((8,)),
        pltpu.SemaphoreType.DMA((TRANSFERS,)),
        pltpu.SemaphoreType.DMA((TRANSFERS,)),
    ]
    child_x, root_x = pl.pallas_call(
        kernel,
        out_shape=(
            jax.ShapeDtypeStruct((8, 64, 256), BF16),
            jax.ShapeDtypeStruct((6, 256, 256), BF16),
        ),
        in_specs=[away] * 5 + [near],
        out_specs=(away, away),
        scratch_shapes=scratch,
        compiler_params=pltpu.CompilerParams(
            collective_id=0, has_side_effects=True, vmem_limit_bytes=60 * 1024 * 1024
        ),
        cost_estimate=pl.CostEstimate(flops=3_000_000_000, bytes_accessed=10_000_000, transcendentals=0),
        name="substitution",
    )(child, rhs, link, root, root_rhs[:, 0], structure)
    child_x = child_x.reshape(2, 256, 256).astype(F32)
    return child_x[None, :, None], root_x.astype(F32)[:, None]


def solution(mesh):
    placed = (
        P("leaf", None, "col", None, None),
        P("leaf", None, "row", None, None, "col", None),
        P(None, "row", None, None, "col", None),
        P("leaf", None, "row", None, None, "col", None),
        P(None, "col", None, None),
        P("leaf", None),
    )
    return jax.shard_map(
        on_device,
        mesh=mesh,
        in_specs=placed,
        out_specs=(P("leaf", None, "col", None, None), P(None, "col", None, None)),
        check_vma=False,
    )
```

```python
import jax
import jax.numpy as jnp
from jax import lax
from jax.experimental import pallas as pl
from jax.experimental.pallas import tpu as pltpu
from jax.sharding import PartitionSpec as P

F32 = jnp.float32
BF16 = jnp.bfloat16
MESH = pl.DeviceIdType.MESH

N_XZ, C_RS, A_AG, D_RS, D_AG = range(0, 10, 2)
F_RS, F_AG, L_XZ, L_C, U_AG, Y_RS, Y_AG, X_RS, X_C, S_X, O_AG, O_X = range(10, 22)
TRANSFERS = 22
HALVES = (0, 1)
FAR_FIRST = (4, 3, 5, 2, 6, 1, 7)


def swap_halves(v):
    flat = v.reshape(-1, 128)
    return pltpu.roll(flat, 64, 1).reshape(v.shape)


def left_half(shape):
    return lax.broadcasted_iota(jnp.int32, shape, len(shape) - 1) < 64


def pack_quarters(top, bottom):
    left = left_half(top.shape)
    return jnp.where(left, top, swap_halves(bottom)), jnp.where(left, swap_halves(top), bottom)


def kernel(
    child, rhs, link_h, root_h, root_rhs_h, structure_h,
    child_out, root_out,
    link, root, root_rhs, child_t, link_t, root_t,
    f_send, f_recv, f_mine, f_all, l_send, l_recv, lx_all, c_send, c_recv,
    u_all, spread, y_send, y_recv, y_all, x_send, x_recv, x_all, n_send, n_recv, n_all,
    c2_send, c2_recv, a_all, d_send, d_recv, d_all, o_all, o_recv,
    ids_v, ids, local_sem, send_sem, recv_sem,
):
    leaf, row, col = (lax.axis_index(a) for a in ("leaf", "row", "col"))
    place = {"leaf": leaf, "row": row, "col": col}
    size = {"leaf": 4, "row": 8, "col": 8}
    sends = []

    def peer(axis, step):
        return lax.rem(place[axis] + step, size[axis])

    def copy(number, arrival, source, target, device):
        return pltpu.make_async_remote_copy(
            src_ref=source, dst_ref=target,
            send_sem=send_sem.at[number], recv_sem=recv_sem.at[arrival],
            device_id=device, device_id_type=MESH,
        )

    def start(number, axis, source, target, whole):
        for step in FAR_FIRST if size[axis] == 8 else (2, 1, 3):
            there = peer(axis, step)
            copy(number, number, source(there), target(step), {axis: there}).start()
        pending = copy(number, number, whole, whole, {axis: peer(axis, 1)})
        sends.append(pending)
        return pending

    def scatter(number, axis, parts, landing):
        return start(
            number, axis, lambda there: parts.at[there], lambda step: landing.at[step], parts.at[pl.ds(0, size[axis] - 1)]
        )

    def gather(number, axis, whole):
        mine = whole.at[place[axis]]
        return start(number, axis, lambda there: mine, lambda step: mine, whole.at[pl.ds(0, size[axis] - 1)])

    def arrived(pending):
        pending.wait_recv()

    def total(axis, parts, landing):
        value = parts[place[axis]].astype(F32)
        for step in range(1, size[axis]):
            value = value + landing[step].astype(F32)
        return value

    def dot(a, b):
        return jnp.dot(a, b, preferred_element_type=F32)

    loads = [
        pltpu.make_async_copy(src, dst, local_sem.at[n])
        for n, (src, dst) in enumerate(
            (
                (structure_h, ids_v.at[leaf]), (link_h, link), (root_rhs_h, root_rhs), (root_h, root),
            )
        )
    ]
    loads[0].start()
    barrier = pltpu.get_barrier_semaphore()
    for step in range(1, 8):
        pl.semaphore_signal(barrier, inc=1, device_id={"col": peer("col", step)}, device_id_type=MESH)
    for step in range(1, 32):
        there = {"leaf": peer("leaf", step // 8), "row": peer("row", step % 8)}
        pl.semaphore_signal(barrier, inc=1, device_id=there, device_id_type=MESH)

    for a in range(2):
        part = dot(child[a, 0], rhs[0]) + dot(child[a, 1], rhs[1])
        f_send[pl.ds(4 * a, 4)] = part.reshape(4, 64, 256).astype(BF16)
    pl.semaphore_wait(barrier, 38)
    pending = scatter(F_RS, "col", f_send, f_recv)
    for load in loads[1:]:
        load.start()
    loads[0].wait()
    mine = ids_v.at[leaf]
    structure_pending = start(
        S_X, "leaf", lambda there: structure_h, lambda step: ids_v.at[leaf], ids_v.at[pl.ds(0, 3)]
    )
    loads[1].wait()
    for a in range(2):
        for m in range(3):
            link_t[m, a] = link[a, m].T
    arrived(pending)
    f_mine[...] = total("col", f_send, f_recv)
    f_all[col] = f_mine[...].astype(BF16)
    pending = gather(F_AG, "col", f_all)
    for a in range(2):
        for x in range(2):
            child_t[x, a] = child[a, x].T
    arrived(pending)

    for h in HALVES:
        for m in range(3):
            part = jnp.zeros((256, 128), F32)
            for a in range(2):
                part = part + dot(link_t[m, a], f_all[pl.ds(4 * a, 4), :, pl.ds(128 * h, 128)].reshape(256, 128))
            part = part.reshape(8, 2, 16, 128)
            for q, packed in enumerate(pack_quarters(part[:, 0], part[:, 1])):
                l_send[2 * h + q, :, m] = packed.astype(BF16)
        for step in FAR_FIRST:
            for there in (2 * h, 2 * h + 1):
                at = peer("row", step)
                copy(L_XZ, L_XZ, l_send.at[there, at], l_recv.at[leaf * 8 + step], {"leaf": there, "row": at}).start()
    for step in (2, 1, 3):
        there = peer("leaf", step)
        copy(L_XZ, L_XZ, l_send.at[there, row], l_recv.at[leaf * 8], {"leaf": there}).start()
    pltpu.make_async_copy(l_send.at[leaf, row], l_recv.at[leaf * 8], recv_sem.at[L_XZ]).start()
    pending = copy(L_XZ, L_XZ, l_recv.at[pl.ds(0, 31)], l_recv, {"row": peer("row", 1)})
    sends.append(pending)
    loads[2].wait()
    loads[3].wait()

    def turn(n, carry):
        a, x = n // 6, n % 6
        root_t[x * 6 + a] = root[a * 6 + x].T
        return carry

    lax.fori_loop(0, 12, turn, 0)
    arrived(structure_pending)
    to_scalars = pltpu.make_async_copy(ids_v, ids, local_sem.at[6])
    to_scalars.start()
    to_scalars.wait()
    arrived(pending)
    for child_at in range(4):
        value = l_recv[child_at * 8].astype(F32)
        for step in range(1, 8):
            value = value + l_recv[child_at * 8 + step].astype(F32)
        lx_all[child_at] = value

    block = lax.broadcasted_iota(jnp.int32, (6, 16, 128), 0) * 8
    for target in range(8):
        value = jnp.zeros((6, 16, 128), F32)
        for child_at in range(4):
            for m in range(3):
                wanted = ids[child_at, 0, col + 8 * m] - target
                value = value + jnp.where(block == wanted, lx_all[child_at, m][None], 0.0)
        c_send[target] = value.astype(BF16)
    pending = scatter(L_C, "col", c_send, c_recv)
    base = root_rhs[:, pl.ds(pl.multiple_of(row * 32, 32), 32), pl.ds(pl.multiple_of((leaf // 2) * 128, 128), 128)]
    base = base.astype(F32)
    first, second = pack_quarters(base[:, :16], base[:, 16:])
    base = jnp.where(leaf % 2 == 0, first, second)
    arrived(pending)
    u_all[row] = (base - total("col", c_send, c_recv)).astype(BF16)
    pending = gather(U_AG, "row", u_all)
    lax.fori_loop(12, 36, turn, 0)
    left = left_half((8, 16, 128))
    keep_left = jnp.where(left, 1.0, 0.0).astype(BF16)
    keep_right = jnp.where(left, 0.0, 1.0).astype(BF16)

    def spread_out(whole):
        for a in range(6):
            spread[a, :, 0] = whole[:, a] * keep_left
            spread[a, :, 1] = whole[:, a] * keep_right

    def root_product(matrix, parts):
        for a in range(6):
            value = jnp.zeros((256, 128), F32)
            for x in range(6):
                value = value + dot(matrix[a * 6 + x], spread[x].reshape(256, 128))
            value = value + swap_halves(value)
            value = value.reshape(8, 2, 16, 128)
            parts[:, a] = jnp.where(left, value[:, 0], value[:, 1]).astype(BF16)

    arrived(pending)
    spread_out(u_all)
    root_product(root, y_send)
    pending = scatter(Y_RS, "col", y_send, y_recv)
    arrived(pending)
    y_all[col] = total("col", y_send, y_recv).astype(BF16)
    pending = gather(Y_AG, "col", y_all)
    arrived(pending)
    spread_out(y_all)
    root_product(root_t, x_send)
    pending = scatter(X_RS, "row", x_send, x_recv)
    arrived(pending)
    solved = total("row", x_send, x_recv).astype(BF16)
    x_all[col] = solved
    pending = gather(X_C, "col", x_all)
    o_all[row] = solved
    arrived(pending)

    for child_at in range(4):
        for m in range(3):
            r = ids[child_at, 0, col + 8 * m]
            n_send[child_at, m] = x_all[r & 7, r >> 3]
    half_at = N_XZ + leaf // 2
    for step in FAR_FIRST + (0,):
        for leaf_step in (0, 1, 2, 3) if step else (1, 2, 3):
            there, at = peer("leaf", leaf_step), peer("row", step)
            copy(N_XZ, half_at, n_send.at[there], n_recv.at[leaf, row], {"leaf": there, "row": at}).start()
    pltpu.make_async_copy(n_send.at[leaf], n_recv.at[leaf, row], recv_sem.at[half_at]).start()
    sends.append(copy(N_XZ, N_XZ, l_recv.at[pl.ds(0, 31)], l_recv, {"row": peer("row", 1)}))

    def unpack(even, odd):
        even, odd = even.astype(F32), odd.astype(F32)
        mask = left_half(even.shape)
        top = jnp.where(mask, even, swap_halves(odd))
        bottom = jnp.where(mask, swap_halves(even), odd)
        return top.astype(BF16), bottom.astype(BF16)

    flight = {}
    for h in HALVES:
        pieces = n_recv.at[pl.ds(2 * h, 2)]
        arrived(copy(N_XZ, N_XZ + h, pieces, pieces, {"row": peer("row", 1)}))
        for m in range(3):
            n_all[m, :, 0], n_all[m, :, 1] = unpack(n_recv[2 * h, :, m], n_recv[2 * h + 1, :, m])
        for a in range(2):
            part = jnp.zeros((256, 128), F32)
            for m in range(3):
                part = part + dot(link[a, m], n_all[m].reshape(256, 128))
            c2_send[h, pl.ds(4 * a, 4)] = part.reshape(4, 64, 128).astype(BF16)
        flight[h] = scatter(C_RS + h, "col", c2_send.at[h], c2_recv.at[h])
    out_pending = gather(O_AG, "row", o_all)
    for h in HALVES:
        arrived(flight[h])
        carried = total("col", c2_send.at[h], c2_recv.at[h])
        a_all[h, col] = (f_mine[:, pl.ds(128 * h, 128)] - carried).astype(BF16)
        flight[h] = gather(A_AG + h, "col", a_all.at[h])

    for h in HALVES:
        arrived(flight[h])
        for x in range(2):
            part = jnp.zeros((256, 128), F32)
            for a in range(2):
                part = part + dot(child_t[x, a], a_all[h, pl.ds(4 * a, 4)].reshape(256, 128))
            d_send[h, pl.ds(4 * x, 4)] = part.reshape(4, 64, 128).astype(BF16)
        flight[h] = scatter(D_RS + h, "row", d_send.at[h], d_recv.at[h])
    arrived(out_pending)
    o_recv[leaf] = o_all[...]
    out_pending = start(O_X, "leaf", lambda there: o_all, lambda step: o_recv.at[leaf], o_recv.at[pl.ds(0, 3)])
    for h in HALVES:
        arrived(flight[h])
        d_all[h, row] = total("row", d_send.at[h], d_recv.at[h]).astype(BF16)
        flight[h] = gather(D_AG + h, "row", d_all.at[h])
    arrived(out_pending)
    for h in HALVES:
        for r in range(8):
            top, bottom = unpack(o_recv[2 * h, r], o_recv[2 * h + 1, r])
            root_out[:, pl.ds(32 * r, 16), pl.ds(128 * h, 128)] = top
            root_out[:, pl.ds(32 * r + 16, 16), pl.ds(128 * h, 128)] = bottom
    for h in HALVES:
        arrived(flight[h])
        child_out[:, :, pl.ds(128 * h, 128)] = d_all[h]
    for pending in sends:
        pending.wait_send()


def on_device(child_rhs, child_inv, root_inv, coupling, root_rhs, structure):
    child = child_inv[0, :, 0, :, :, 0, :].transpose(0, 2, 1, 3)
    rhs = child_rhs[0, :, 0]
    link = coupling[0, :, 0, :, :, 0, :].transpose(0, 2, 1, 3)
    root = root_inv[:, 0, :, :, 0, :].transpose(0, 2, 1, 3).reshape(36, 256, 256)
    away = pl.BlockSpec(memory_space=pltpu.HBM)
    near = pl.BlockSpec(memory_space=pltpu.VMEM)
    packed = (6, 16, 128)
    half = (2, 8, 64, 128)
    shapes = [
        (2, 3, 256, 256), (36, 256, 256), (6, 256, 256),
        (2, 2, 256, 256), (3, 2, 256, 256), (36, 256, 256),
        (8, 64, 256), (8, 64, 256), None, (8, 64, 256),
        (4, 8, 3, 16, 128), (32, 3, 16, 128), None, (8,) + packed, (8,) + packed,
        (8,) + packed, (6, 8, 2, 16, 128),
        (8,) + packed, (8,) + packed, (8,) + packed,
        (8,) + packed, (8,) + packed, (8,) + packed,
        (4, 3, 16, 128), (4, 8, 3, 16, 128), (3, 8, 2, 16, 128),
        half, half, half,
        half, half, half,
        (8,) + packed, (4, 8) + packed,
    ]
    wide = iter([(64, 256), (4, 3, 16, 128)])
    scratch = [
        pltpu.VMEM(next(wide), F32) if shape is None else pltpu.VMEM(shape, BF16) for shape in shapes
    ]
    scratch += [
        pltpu.VMEM((4, 1, 24), jnp.int32),
        pltpu.SMEM((4, 1, 24), jnp.int32),
        pltpu.SemaphoreType.DMA((7,)),
        pltpu.SemaphoreType.DMA((TRANSFERS,)),
        pltpu.SemaphoreType.DMA((TRANSFERS,)),
    ]
    child_x, root_x = pl.pallas_call(
        kernel,
        out_shape=(
            jax.ShapeDtypeStruct((8, 64, 256), BF16),
            jax.ShapeDtypeStruct((6, 256, 256), BF16),
        ),
        in_specs=[near] * 2 + [away] * 4,
        out_specs=(near, near),
        scratch_shapes=scratch,
        compiler_params=pltpu.CompilerParams(
            collective_id=0, has_side_effects=True, vmem_limit_bytes=207 * 256 * 1024
        ),
        cost_estimate=pl.CostEstimate(flops=3_000_000_000, bytes_accessed=10_000_000, transcendentals=0),
        name="substitution",
    )(child, rhs, link, root, root_rhs[:, 0], structure)
    child_x = child_x.reshape(2, 256, 256).astype(F32)
    return child_x[None, :, None], root_x.astype(F32)[:, None]


def solution(mesh):
    placed = (
        P("leaf", None, "col", None, None),
        P("leaf", None, "row", None, None, "col", None),
        P(None, "row", None, None, "col", None),
        P("leaf", None, "row", None, None, "col", None),
        P(None, "col", None, None),
        P("leaf", None),
    )
    return jax.shard_map(
        on_device,
        mesh=mesh,
        in_specs=placed,
        out_specs=(P("leaf", None, "col", None, None), P(None, "col", None, None)),
        check_vma=False,
    )
```

```python
import jax
import jax.numpy as jnp
from jax import lax
from jax.experimental import pallas as pl
from jax.experimental.pallas import tpu as pltpu
from jax.sharding import PartitionSpec as P

F32 = jnp.float32
BF16 = jnp.bfloat16
MESH = pl.DeviceIdType.MESH

N_XZ, C_CORE, C_Y, A_CORE, D_RS, D_AG = range(0, 12, 2)
F_RS, F_AG, L_XZ, L_C, U_AG, Y_CORE, Y_Y, Y_BACK, X_RS, X_C, S_X, O_AG, O_X = range(12, 25)
TRANSFERS = 25
HALVES = (0, 1)
FAR_FIRST = (4, 3, 5, 2, 6, 1, 7)


def swap_halves(v):
    flat = v.reshape(-1, 128)
    return pltpu.roll(flat, 64, 1).reshape(v.shape)


def left_half(shape):
    return lax.broadcasted_iota(jnp.int32, shape, len(shape) - 1) < 64


def pack_quarters(top, bottom):
    left = left_half(top.shape)
    return jnp.where(left, top, swap_halves(bottom)), jnp.where(left, swap_halves(top), bottom)


def kernel(
    child, rhs, link_h, root_h, root_rhs_h, structure_h,
    child_out, root_out,
    link, root, root_rhs, child_t, link_t, root_t,
    f_send, f_recv, f_all, l_send, l_recv, lx_all, c_send, c_recv,
    u_all, spread, y_send, y_recv, y_pairs, y_all, x_send, x_recv, x_all, n_send, n_recv, n_all,
    c2_send, c2_recv, c2_pairs, a_all, d_send, d_recv, d_all, o_all, o_recv,
    ids_v, ids, local_sem, send_sem, recv_sem,
):
    leaf, row, col = (lax.axis_index(a) for a in ("leaf", "row", "col"))
    place = {"leaf": leaf, "row": row, "col": col}
    size = {"leaf": 4, "row": 8, "col": 8}
    core, chip = lax.rem(col, 2), col // 2
    other = {"col": col + 1 - 2 * core}
    sends = []

    def peer(axis, step):
        return lax.rem(place[axis] + step, size[axis])

    def copy(number, arrival, source, target, device):
        return pltpu.make_async_remote_copy(
            src_ref=source, dst_ref=target,
            send_sem=send_sem.at[number], recv_sem=recv_sem.at[arrival],
            device_id=device, device_id_type=MESH,
        )

    def start(number, axis, source, target, whole):
        for step in FAR_FIRST if size[axis] == 8 else (2, 1, 3):
            there = peer(axis, step)
            copy(number, number, source(there), target(step), {axis: there}).start()
        pending = copy(number, number, whole, whole, {axis: peer(axis, 1)})
        sends.append(pending)
        return pending

    def scatter(number, axis, parts, landing):
        return start(
            number, axis, lambda there: parts.at[there], lambda step: landing.at[step], parts.at[pl.ds(0, size[axis] - 1)]
        )

    def gather(number, axis, whole):
        mine = whole.at[place[axis]]
        return start(number, axis, lambda there: mine, lambda step: mine, whole.at[pl.ds(0, size[axis] - 1)])

    def to_other_core(number, source, target):
        pending = copy(number, number, source, target, other)
        pending.start()
        sends.append(pending)
        return pending

    def to_other_chips(number, whole):
        mine = whole.at[chip]
        for step in (2, 1, 3):
            copy(number, number, mine, mine, {"col": 2 * lax.rem(chip + step, 4) + core}).start()
        pending = copy(number, number, whole.at[pl.ds(0, 3)], whole.at[pl.ds(0, 3)], other)
        sends.append(pending)
        return pending

    def over_chips(whole):
        return (whole[0].astype(F32) + whole[1].astype(F32)) + (whole[2].astype(F32) + whole[3].astype(F32))

    def arrived(pending):
        pending.wait_recv()

    def total(axis, parts, landing):
        value = parts[place[axis]].astype(F32)
        for step in range(1, size[axis]):
            value = value + landing[step].astype(F32)
        return value

    def dot(a, b):
        return jnp.dot(a, b, preferred_element_type=F32)

    loads = [
        pltpu.make_async_copy(src, dst, local_sem.at[n])
        for n, (src, dst) in enumerate(
            (
                (structure_h, ids_v.at[leaf]), (link_h, link), (root_rhs_h, root_rhs), (root_h, root),
            )
        )
    ]
    loads[0].start()
    barrier = pltpu.get_barrier_semaphore()
    for step in range(1, 8):
        pl.semaphore_signal(barrier, inc=1, device_id={"col": peer("col", step)}, device_id_type=MESH)
    for step in range(1, 32):
        there = {"leaf": peer("leaf", step // 8), "row": peer("row", step % 8)}
        pl.semaphore_signal(barrier, inc=1, device_id=there, device_id_type=MESH)

    for a in range(2):
        part = dot(child[a, 0], rhs[0]) + dot(child[a, 1], rhs[1])
        f_send[pl.ds(4 * a, 4)] = part.reshape(4, 64, 256).astype(BF16)
    pl.semaphore_wait(barrier, 38)
    pending = scatter(F_RS, "col", f_send, f_recv)
    for load in loads[1:]:
        load.start()
    loads[0].wait()
    mine = ids_v.at[leaf]
    structure_pending = start(
        S_X, "leaf", lambda there: structure_h, lambda step: ids_v.at[leaf], ids_v.at[pl.ds(0, 3)]
    )
    loads[1].wait()
    for a in range(2):
        for m in range(3):
            link_t[m, a] = link[a, m].T
    arrived(pending)
    f_all[col] = total("col", f_send, f_recv).astype(BF16)
    pending = gather(F_AG, "col", f_all)
    for a in range(2):
        for x in range(2):
            child_t[x, a] = child[a, x].T
    arrived(pending)

    for h in HALVES:
        for m in range(3):
            part = jnp.zeros((256, 128), F32)
            for a in range(2):
                part = part + dot(link_t[m, a], f_all[pl.ds(4 * a, 4), :, pl.ds(128 * h, 128)].reshape(256, 128))
            part = part.reshape(8, 2, 16, 128)
            for q, packed in enumerate(pack_quarters(part[:, 0], part[:, 1])):
                l_send[2 * h + q, :, m] = packed.astype(BF16)
    for leaf_step in (2, 1, 3, 0):
        for step in FAR_FIRST + ((0,) if leaf_step else ()):
            there, at = peer("leaf", leaf_step), peer("row", step)
            copy(L_XZ, L_XZ, l_send.at[there, at], l_recv.at[leaf * 8 + step], {"leaf": there, "row": at}).start()
    pltpu.make_async_copy(l_send.at[leaf, row], l_recv.at[leaf * 8], recv_sem.at[L_XZ]).start()
    pending = copy(L_XZ, L_XZ, l_recv.at[pl.ds(0, 31)], l_recv, {"row": peer("row", 1)})
    sends.append(pending)
    loads[2].wait()
    loads[3].wait()

    def turn(n, carry):
        a, x = n // 6, n % 6
        root_t[x * 6 + a] = root[a * 6 + x].T
        return carry

    lax.fori_loop(0, 12, turn, 0)
    arrived(structure_pending)
    to_scalars = pltpu.make_async_copy(ids_v, ids, local_sem.at[6])
    to_scalars.start()
    to_scalars.wait()
    arrived(pending)
    for child_at in range(4):
        value = l_recv[child_at * 8].astype(F32)
        for step in range(1, 8):
            value = value + l_recv[child_at * 8 + step].astype(F32)
        lx_all[child_at] = value

    block = lax.broadcasted_iota(jnp.int32, (6, 16, 128), 0) * 8
    for target in range(8):
        value = jnp.zeros((6, 16, 128), F32)
        for child_at in range(4):
            for m in range(3):
                wanted = ids[child_at, 0, col + 8 * m] - target
                value = value + jnp.where(block == wanted, lx_all[child_at, m][None], 0.0)
        c_send[target] = value.astype(BF16)
    pending = scatter(L_C, "col", c_send, c_recv)
    base = root_rhs[:, pl.ds(pl.multiple_of(row * 32, 32), 32), pl.ds(pl.multiple_of((leaf // 2) * 128, 128), 128)]
    base = base.astype(F32)
    first, second = pack_quarters(base[:, :16], base[:, 16:])
    base = jnp.where(leaf % 2 == 0, first, second)
    arrived(pending)
    u_all[row] = (base - total("col", c_send, c_recv)).astype(BF16)
    pending = gather(U_AG, "row", u_all)
    lax.fori_loop(12, 36, turn, 0)
    left = left_half((8, 16, 128))
    keep_left = jnp.where(left, 1.0, 0.0).astype(BF16)
    keep_right = jnp.where(left, 0.0, 1.0).astype(BF16)

    def spread_out(whole):
        for a in range(6):
            spread[a, :, 0] = whole[:, a] * keep_left
            spread[a, :, 1] = whole[:, a] * keep_right

    def root_product(matrix, parts):
        for a in range(6):
            value = jnp.zeros((256, 128), F32)
            for x in range(6):
                value = value + dot(matrix[a * 6 + x], spread[x].reshape(256, 128))
            value = value + swap_halves(value)
            value = value.reshape(8, 2, 16, 128)
            parts[:, a] = jnp.where(left, value[:, 0], value[:, 1]).astype(parts.dtype)

    arrived(pending)
    spread_out(u_all)
    root_product(root, y_send)
    mine, theirs = pl.ds(4 * core, 4), pl.ds(4 - 4 * core, 4)
    pending = to_other_core(Y_CORE, y_send.at[theirs], y_recv)
    arrived(pending)
    y_pairs[chip] = (y_send[mine] + y_recv[...]).astype(BF16)
    pending = to_other_chips(Y_Y, y_pairs)
    arrived(pending)
    y_all[mine] = over_chips(y_pairs).astype(BF16)
    pending = to_other_core(Y_BACK, y_all.at[mine], y_all.at[mine])
    arrived(pending)
    spread_out(y_all)
    root_product(root_t, x_send)
    pending = scatter(X_RS, "row", x_send, x_recv)
    arrived(pending)
    solved = total("row", x_send, x_recv).astype(BF16)
    x_all[col] = solved
    pending = gather(X_C, "col", x_all)
    o_all[row] = solved
    arrived(pending)

    for child_at in range(4):
        for m in range(3):
            r = ids[child_at, 0, col + 8 * m]
            n_send[child_at, m] = x_all[r & 7, r >> 3]
    half_at = N_XZ + leaf // 2
    for leaf_step in (2, 1, 3, 0):
        for step in FAR_FIRST + ((0,) if leaf_step else ()):
            there, at = peer("leaf", leaf_step), peer("row", step)
            copy(N_XZ, half_at, n_send.at[there], n_recv.at[leaf, row], {"leaf": there, "row": at}).start()
    pltpu.make_async_copy(n_send.at[leaf], n_recv.at[leaf, row], recv_sem.at[half_at]).start()
    sends.append(copy(N_XZ, N_XZ, l_recv.at[pl.ds(0, 31)], l_recv, {"row": peer("row", 1)}))

    def unpack(even, odd):
        even, odd = even.astype(F32), odd.astype(F32)
        mask = left_half(even.shape)
        top = jnp.where(mask, even, swap_halves(odd))
        bottom = jnp.where(mask, swap_halves(even), odd)
        return top.astype(BF16), bottom.astype(BF16)

    flight = {}
    for h in HALVES:
        pieces = n_recv.at[pl.ds(2 * h, 2)]
        arrived(copy(N_XZ, N_XZ + h, pieces, pieces, {"row": peer("row", 1)}))
        for m in range(3):
            n_all[m, :, 0], n_all[m, :, 1] = unpack(n_recv[2 * h, :, m], n_recv[2 * h + 1, :, m])
        for n, a in enumerate((1 - core, core)):
            part = jnp.zeros((256, 128), F32)
            for m in range(3):
                part = part + dot(link[a, m], n_all[m].reshape(256, 128))
            c2_send[h, n] = part
            if n == 0:
                flight[h] = to_other_core(C_CORE + h, c2_send.at[h, 0], c2_recv.at[h])
    out_pending = gather(O_AG, "row", o_all)
    for h in HALVES:
        arrived(flight[h])
        c2_pairs[h, chip] = (c2_send[h, 1] + c2_recv[h]).astype(BF16)
        flight[h] = to_other_chips(C_Y + h, c2_pairs.at[h])
    for h in HALVES:
        arrived(flight[h])
        known = f_all[pl.ds(4 * core, 4), :, pl.ds(128 * h, 128)].astype(F32)
        a_all[h, core] = (known.reshape(256, 128) - over_chips(c2_pairs.at[h])).astype(BF16)
        flight[h] = to_other_core(A_CORE + h, a_all.at[h, core], a_all.at[h, core])

    for h in HALVES:
        arrived(flight[h])
        for x in range(2):
            part = jnp.zeros((256, 128), F32)
            for a in range(2):
                part = part + dot(child_t[x, a], a_all[h, a])
            d_send[h, pl.ds(4 * x, 4)] = part.reshape(4, 64, 128).astype(BF16)
        flight[h] = scatter(D_RS + h, "row", d_send.at[h], d_recv.at[h])
    arrived(out_pending)
    o_recv[leaf] = o_all[...]
    out_pending = start(O_X, "leaf", lambda there: o_all, lambda step: o_recv.at[leaf], o_recv.at[pl.ds(0, 3)])
    for h in HALVES:
        arrived(flight[h])
        d_all[h, row] = total("row", d_send.at[h], d_recv.at[h]).astype(BF16)
        flight[h] = gather(D_AG + h, "row", d_all.at[h])
    arrived(out_pending)
    for h in HALVES:
        for r in range(8):
            top, bottom = unpack(o_recv[2 * h, r], o_recv[2 * h + 1, r])
            root_out[:, pl.ds(32 * r, 16), pl.ds(128 * h, 128)] = top
            root_out[:, pl.ds(32 * r + 16, 16), pl.ds(128 * h, 128)] = bottom
    for h in HALVES:
        arrived(flight[h])
        child_out[:, :, pl.ds(128 * h, 128)] = d_all[h]
    for pending in sends:
        pending.wait_send()


def on_device(child_rhs, child_inv, root_inv, coupling, root_rhs, structure):
    child = child_inv[0, :, 0, :, :, 0, :].transpose(0, 2, 1, 3)
    rhs = child_rhs[0, :, 0]
    link = coupling[0, :, 0, :, :, 0, :].transpose(0, 2, 1, 3)
    root = root_inv[:, 0, :, :, 0, :].transpose(0, 2, 1, 3).reshape(36, 256, 256)
    away = pl.BlockSpec(memory_space=pltpu.HBM)
    near = pl.BlockSpec(memory_space=pltpu.VMEM)
    packed = (6, 16, 128)
    half = (2, 8, 64, 128)
    shapes = [
        (2, 3, 256, 256), (36, 256, 256), (6, 256, 256),
        (2, 2, 256, 256), (3, 2, 256, 256), (36, 256, 256),
        (8, 64, 256), (8, 64, 256), (8, 64, 256),
        (4, 8, 3, 16, 128), (32, 3, 16, 128), pltpu.VMEM((4, 3, 16, 128), F32), (8,) + packed, (8,) + packed,
        (8,) + packed, (6, 8, 2, 16, 128),
        pltpu.VMEM((8,) + packed, F32), pltpu.VMEM((4,) + packed, F32), (4, 4) + packed, (8,) + packed,
        (8,) + packed, (8,) + packed, (8,) + packed,
        (4, 3, 16, 128), (4, 8, 3, 16, 128), (3, 8, 2, 16, 128),
        pltpu.VMEM((2, 2, 256, 128), F32), pltpu.VMEM((2, 256, 128), F32), (2, 4, 256, 128), (2, 2, 256, 128),
        half, half, half,
        (8,) + packed, (4, 8) + packed,
    ]
    scratch = [pltpu.VMEM(s, BF16) if isinstance(s, tuple) else s for s in shapes]
    scratch += [
        pltpu.VMEM((4, 1, 24), jnp.int32),
        pltpu.SMEM((4, 1, 24), jnp.int32),
        pltpu.SemaphoreType.DMA((7,)),
        pltpu.SemaphoreType.DMA((TRANSFERS,)),
        pltpu.SemaphoreType.DMA((TRANSFERS,)),
    ]
    child_x, root_x = pl.pallas_call(
        kernel,
        out_shape=(
            jax.ShapeDtypeStruct((8, 64, 256), BF16),
            jax.ShapeDtypeStruct((6, 256, 256), BF16),
        ),
        in_specs=[near] * 2 + [away] * 4,
        out_specs=(near, near),
        scratch_shapes=scratch,
        compiler_params=pltpu.CompilerParams(
            collective_id=0, has_side_effects=True, vmem_limit_bytes=207 * 256 * 1024
        ),
        cost_estimate=pl.CostEstimate(flops=3_000_000_000, bytes_accessed=10_000_000, transcendentals=0),
        name="substitution",
    )(child, rhs, link, root, root_rhs[:, 0], structure)
    child_x = child_x.reshape(2, 256, 256).astype(F32)
    return child_x[None, :, None], root_x.astype(F32)[:, None]


def solution(mesh):
    placed = (
        P("leaf", None, "col", None, None),
        P("leaf", None, "row", None, None, "col", None),
        P(None, "row", None, None, "col", None),
        P("leaf", None, "row", None, None, "col", None),
        P(None, "col", None, None),
        P("leaf", None),
    )
    return jax.shard_map(
        on_device,
        mesh=mesh,
        in_specs=placed,
        out_specs=(P("leaf", None, "col", None, None), P(None, "col", None, None)),
        check_vma=False,
    )
```

```python
import jax
import jax.numpy as jnp
from jax import lax
from jax.experimental import pallas as pl
from jax.experimental.pallas import tpu as pltpu
from jax.sharding import PartitionSpec as P

F32 = jnp.float32
BF16 = jnp.bfloat16
MESH = pl.DeviceIdType.MESH

N_XZ, C_RS, A_AG, D_RS, D_AG = range(0, 10, 2)
F_RS, F_AG, L_XZ, L_C, U_AG, Y_RS, Y_AG, X_RS, X_C, S_X, O_AG, O_X = range(10, 22)
TRANSFERS = 22
HALVES = (0, 1)
FAR_FIRST = (4, 3, 5, 2, 6, 1, 7)


def swap_halves(v):
    flat = v.reshape(-1, 128)
    return pltpu.roll(flat, 64, 1).reshape(v.shape)


def left_half(shape):
    return lax.broadcasted_iota(jnp.int32, shape, len(shape) - 1) < 64


def pack_quarters(top, bottom):
    left = left_half(top.shape)
    return jnp.where(left, top, swap_halves(bottom)), jnp.where(left, swap_halves(top), bottom)


def kernel(
    child_h, rhs_h, link_h, root_h, root_rhs_h, structure_h,
    child_out_h, root_out_h,
    raw, child, rhs, link, root, root_rhs, child_t, link_t, root_t,
    f_send, f_recv, f_mine, f_all, l_send, l_recv, lx_all, c_send, c_recv,
    u_all, spread, y_send, y_recv, y_all, x_send, x_recv, x_all, n_send, n_recv, n_all,
    c2_send, c2_recv, a_all, d_send, d_recv, d_all, o_all, o_recv, root_out,
    ids_v, ids, local_sem, send_sem, recv_sem,
):
    leaf, row, col = (lax.axis_index(a) for a in ("leaf", "row", "col"))
    place = {"leaf": leaf, "row": row, "col": col}
    size = {"leaf": 4, "row": 8, "col": 8}
    sends = []

    def peer(axis, step):
        return lax.rem(place[axis] + step, size[axis])

    def copy(number, arrival, source, target, device):
        return pltpu.make_async_remote_copy(
            src_ref=source, dst_ref=target,
            send_sem=send_sem.at[number], recv_sem=recv_sem.at[arrival],
            device_id=device, device_id_type=MESH,
        )

    def start(number, axis, source, target, whole):
        for step in FAR_FIRST if size[axis] == 8 else (2, 1, 3):
            there = peer(axis, step)
            copy(number, number, source(there), target(step), {axis: there}).start()
        pending = copy(number, number, whole, whole, {axis: peer(axis, 1)})
        sends.append(pending)
        return pending

    def scatter(number, axis, parts, landing):
        return start(
            number, axis, lambda there: parts.at[there], lambda step: landing.at[step], parts.at[pl.ds(0, size[axis] - 1)]
        )

    def gather(number, axis, whole):
        mine = whole.at[place[axis]]
        return start(number, axis, lambda there: mine, lambda step: mine, whole.at[pl.ds(0, size[axis] - 1)])

    def arrived(pending):
        pending.wait_recv()

    def total(axis, parts, landing):
        value = parts[place[axis]].astype(F32)
        for step in range(1, size[axis]):
            value = value + landing[step].astype(F32)
        return value

    def dot(a, b):
        return jnp.dot(a, b, preferred_element_type=F32)

    loads = [
        pltpu.make_async_copy(src, dst, local_sem.at[n])
        for n, (src, dst) in enumerate(
            (
                (structure_h, ids_v.at[leaf]), (child_h, raw), (rhs_h, rhs), (link_h, link), (root_rhs_h, root_rhs), (root_h, root),
            )
        )
    ]
    for n in (1, 2, 0):
        loads[n].start()
    barrier = pltpu.get_barrier_semaphore()
    for step in range(1, 8):
        pl.semaphore_signal(barrier, inc=1, device_id={"col": peer("col", step)}, device_id_type=MESH)
    for step in range(1, 32):
        there = {"leaf": peer("leaf", step // 8), "row": peer("row", step % 8)}
        pl.semaphore_signal(barrier, inc=1, device_id=there, device_id_type=MESH)

    loads[1].wait()
    for a in range(2):
        for x in range(2):
            child[a, x] = raw[a, :, x, :]
    loads[2].wait()
    for a in range(2):
        part = dot(child[a, 0], rhs[0]) + dot(child[a, 1], rhs[1])
        f_send[pl.ds(4 * a, 4)] = part.reshape(4, 64, 256).astype(BF16)
    pl.semaphore_wait(barrier, 38)
    pending = scatter(F_RS, "col", f_send, f_recv)
    for load in loads[3:]:
        load.start()
    loads[0].wait()
    mine = ids_v.at[leaf]
    structure_pending = start(
        S_X, "leaf", lambda there: structure_h, lambda step: ids_v.at[leaf], ids_v.at[pl.ds(0, 3)]
    )
    loads[3].wait()
    for a in range(2):
        for m in range(3):
            link_t[m, a] = link[a, m].T
    arrived(pending)
    f_mine[...] = total("col", f_send, f_recv)
    f_all[col] = f_mine[...].astype(BF16)
    pending = gather(F_AG, "col", f_all)
    for a in range(2):
        for x in range(2):
            child_t[x, a] = child[a, x].T
    arrived(pending)

    for h in HALVES:
        for m in range(3):
            part = jnp.zeros((256, 128), F32)
            for a in range(2):
                part = part + dot(link_t[m, a], f_all[pl.ds(4 * a, 4), :, pl.ds(128 * h, 128)].reshape(256, 128))
            part = part.reshape(8, 2, 16, 128)
            for q, packed in enumerate(pack_quarters(part[:, 0], part[:, 1])):
                l_send[2 * h + q, :, m] = packed.astype(BF16)
    for leaf_step in (2, 1, 3, 0):
        for step in FAR_FIRST + ((0,) if leaf_step else ()):
            there, at = peer("leaf", leaf_step), peer("row", step)
            copy(L_XZ, L_XZ, l_send.at[there, at], l_recv.at[leaf * 8 + step], {"leaf": there, "row": at}).start()
    pltpu.make_async_copy(l_send.at[leaf, row], l_recv.at[leaf * 8], recv_sem.at[L_XZ]).start()
    pending = copy(L_XZ, L_XZ, l_recv.at[pl.ds(0, 31)], l_recv, {"row": peer("row", 1)})
    sends.append(pending)
    loads[4].wait()
    loads[5].wait()

    def turn(n, carry):
        a, x = n // 6, n % 6
        root_t[x * 6 + a] = root[a * 6 + x].T
        return carry

    lax.fori_loop(0, 12, turn, 0)
    arrived(structure_pending)
    to_scalars = pltpu.make_async_copy(ids_v, ids, local_sem.at[8])
    to_scalars.start()
    to_scalars.wait()
    arrived(pending)
    for child_at in range(4):
        value = l_recv[child_at * 8].astype(F32)
        for step in range(1, 8):
            value = value + l_recv[child_at * 8 + step].astype(F32)
        lx_all[child_at] = value

    block = lax.broadcasted_iota(jnp.int32, (6, 16, 128), 0) * 8
    for target in range(8):
        value = jnp.zeros((6, 16, 128), F32)
        for child_at in range(4):
            for m in range(3):
                wanted = ids[child_at, 0, col + 8 * m] - target
                value = value + jnp.where(block == wanted, lx_all[child_at, m][None], 0.0)
        c_send[target] = value.astype(BF16)
    pending = scatter(L_C, "col", c_send, c_recv)
    base = root_rhs[:, pl.ds(pl.multiple_of(row * 32, 32), 32), pl.ds(pl.multiple_of((leaf // 2) * 128, 128), 128)]
    base = base.astype(F32)
    first, second = pack_quarters(base[:, :16], base[:, 16:])
    base = jnp.where(leaf % 2 == 0, first, second)
    arrived(pending)
    u_all[row] = (base - total("col", c_send, c_recv)).astype(BF16)
    pending = gather(U_AG, "row", u_all)
    lax.fori_loop(12, 36, turn, 0)
    left = left_half((8, 16, 128))
    keep_left = jnp.where(left, 1.0, 0.0).astype(BF16)
    keep_right = jnp.where(left, 0.0, 1.0).astype(BF16)

    def spread_out(whole):
        for a in range(6):
            spread[a, :, 0] = whole[:, a] * keep_left
            spread[a, :, 1] = whole[:, a] * keep_right

    def root_product(matrix, parts):
        for a in range(6):
            value = jnp.zeros((256, 128), F32)
            for x in range(6):
                value = value + dot(matrix[a * 6 + x], spread[x].reshape(256, 128))
            value = value + swap_halves(value)
            value = value.reshape(8, 2, 16, 128)
            parts[:, a] = jnp.where(left, value[:, 0], value[:, 1]).astype(BF16)

    arrived(pending)
    spread_out(u_all)
    root_product(root, y_send)
    pending = scatter(Y_RS, "col", y_send, y_recv)
    arrived(pending)
    y_all[col] = total("col", y_send, y_recv).astype(BF16)
    pending = gather(Y_AG, "col", y_all)
    arrived(pending)
    spread_out(y_all)
    root_product(root_t, x_send)
    pending = scatter(X_RS, "row", x_send, x_recv)
    arrived(pending)
    solved = total("row", x_send, x_recv).astype(BF16)
    x_all[col] = solved
    pending = gather(X_C, "col", x_all)
    o_all[row] = solved
    arrived(pending)

    for child_at in range(4):
        for m in range(3):
            r = ids[child_at, 0, col + 8 * m]
            n_send[child_at, m] = x_all[r & 7, r >> 3]
    half_at = N_XZ + leaf // 2
    for step in FAR_FIRST + (0,):
        for leaf_step in (0, 1, 2, 3) if step else (1, 2, 3):
            there, at = peer("leaf", leaf_step), peer("row", step)
            copy(N_XZ, half_at, n_send.at[there], n_recv.at[leaf, row], {"leaf": there, "row": at}).start()
    pltpu.make_async_copy(n_send.at[leaf], n_recv.at[leaf, row], recv_sem.at[half_at]).start()
    sends.append(copy(N_XZ, N_XZ, l_recv.at[pl.ds(0, 31)], l_recv, {"row": peer("row", 1)}))

    def unpack(even, odd):
        even, odd = even.astype(F32), odd.astype(F32)
        mask = left_half(even.shape)
        top = jnp.where(mask, even, swap_halves(odd))
        bottom = jnp.where(mask, swap_halves(even), odd)
        return top.astype(BF16), bottom.astype(BF16)

    flight = {}
    for h in HALVES:
        pieces = n_recv.at[pl.ds(2 * h, 2)]
        arrived(copy(N_XZ, N_XZ + h, pieces, pieces, {"row": peer("row", 1)}))
        for m in range(3):
            n_all[m, :, 0], n_all[m, :, 1] = unpack(n_recv[2 * h, :, m], n_recv[2 * h + 1, :, m])
        for a in range(2):
            part = jnp.zeros((256, 128), F32)
            for m in range(3):
                part = part + dot(link[a, m], n_all[m].reshape(256, 128))
            c2_send[h, pl.ds(4 * a, 4)] = part.reshape(4, 64, 128).astype(BF16)
        flight[h] = scatter(C_RS + h, "col", c2_send.at[h], c2_recv.at[h])
    out_pending = gather(O_AG, "row", o_all)
    for h in HALVES:
        arrived(flight[h])
        carried = total("col", c2_send.at[h], c2_recv.at[h])
        a_all[h, col] = (f_mine[:, pl.ds(128 * h, 128)] - carried).astype(BF16)
        flight[h] = gather(A_AG + h, "col", a_all.at[h])

    for h in HALVES:
        arrived(flight[h])
        for x in range(2):
            part = jnp.zeros((256, 128), F32)
            for a in range(2):
                part = part + dot(child_t[x, a], a_all[h, pl.ds(4 * a, 4)].reshape(256, 128))
            d_send[h, pl.ds(4 * x, 4)] = part.reshape(4, 64, 128).astype(BF16)
        flight[h] = scatter(D_RS + h, "row", d_send.at[h], d_recv.at[h])
    arrived(out_pending)
    o_recv[leaf] = o_all[...]
    out_pending = start(O_X, "leaf", lambda there: o_all, lambda step: o_recv.at[leaf], o_recv.at[pl.ds(0, 3)])
    for h in HALVES:
        arrived(flight[h])
        d_all[h, row] = total("row", d_send.at[h], d_recv.at[h]).astype(BF16)
        flight[h] = gather(D_AG + h, "row", d_all.at[h])
    arrived(out_pending)
    for h in HALVES:
        for r in range(8):
            top, bottom = unpack(o_recv[2 * h, r], o_recv[2 * h + 1, r])
            root_out[:, pl.ds(32 * r, 16), pl.ds(128 * h, 128)] = top
            root_out[:, pl.ds(32 * r + 16, 16), pl.ds(128 * h, 128)] = bottom
    stores = [pltpu.make_async_copy(root_out, root_out_h, local_sem.at[9])]
    stores[0].start()
    for h in HALVES:
        arrived(flight[h])
        store = pltpu.make_async_copy(d_all.at[h], child_out_h.at[:, :, pl.ds(128 * h, 128)], local_sem.at[10 + h])
        store.start()
        stores.append(store)
    for store in stores:
        store.wait()
    for pending in sends:
        pending.wait_send()


def on_device(child_rhs, child_inv, root_inv, coupling, root_rhs, structure):
    child = child_inv[0, :, 0, :, :, 0, :]
    rhs = child_rhs[0, :, 0]
    link = coupling[0, :, 0, :, :, 0, :].transpose(0, 2, 1, 3)
    root = root_inv[:, 0, :, :, 0, :].transpose(0, 2, 1, 3).reshape(36, 256, 256)
    away = pl.BlockSpec(memory_space=pltpu.HBM)
    packed = (6, 16, 128)
    half = (2, 8, 64, 128)
    shapes = [
        (2, 256, 2, 256), (2, 2, 256, 256), (2, 256, 256), (2, 3, 256, 256), (36, 256, 256), (6, 256, 256),
        (2, 2, 256, 256), (3, 2, 256, 256), (36, 256, 256),
        (8, 64, 256), (8, 64, 256), None, (8, 64, 256),
        (4, 8, 3, 16, 128), (32, 3, 16, 128), None, (8,) + packed, (8,) + packed,
        (8,) + packed, (6, 8, 2, 16, 128),
        (8,) + packed, (8,) + packed, (8,) + packed,
        (8,) + packed, (8,) + packed, (8,) + packed,
        (4, 3, 16, 128), (4, 8, 3, 16, 128), (3, 8, 2, 16, 128),
        half, half, half,
        half, half, half,
        (8,) + packed, (4, 8) + packed, (6, 256, 256),
    ]
    wide = iter([(64, 256), (4, 3, 16, 128)])
    scratch = [
        pltpu.VMEM(next(wide), F32) if shape is None else pltpu.VMEM(shape, BF16) for shape in shapes
    ]
    scratch += [
        pltpu.VMEM((4, 1, 24), jnp.int32),
        pltpu.SMEM((4, 1, 24), jnp.int32),
        pltpu.SemaphoreType.DMA((12,)),
        pltpu.SemaphoreType.DMA((TRANSFERS,)),
        pltpu.SemaphoreType.DMA((TRANSFERS,)),
    ]
    child_x, root_x = pl.pallas_call(
        kernel,
        out_shape=(
            jax.ShapeDtypeStruct((8, 64, 256), BF16),
            jax.ShapeDtypeStruct((6, 256, 256), BF16),
        ),
        in_specs=[away] * 6,
        out_specs=(away, away),
        scratch_shapes=scratch,
        compiler_params=pltpu.CompilerParams(
            collective_id=0, has_side_effects=True, vmem_limit_bytes=60 * 1024 * 1024
        ),
        cost_estimate=pl.CostEstimate(flops=3_000_000_000, bytes_accessed=10_000_000, transcendentals=0),
        name="substitution",
    )(child, rhs, link, root, root_rhs[:, 0], structure)
    child_x = child_x.reshape(2, 256, 256).astype(F32)
    return child_x[None, :, None], root_x.astype(F32)[:, None]


def solution(mesh):
    placed = (
        P("leaf", None, "col", None, None),
        P("leaf", None, "row", None, None, "col", None),
        P(None, "row", None, None, "col", None),
        P("leaf", None, "row", None, None, "col", None),
        P(None, "col", None, None),
        P("leaf", None),
    )
    return jax.shard_map(
        on_device,
        mesh=mesh,
        in_specs=placed,
        out_specs=(P("leaf", None, "col", None, None), P(None, "col", None, None)),
        check_vma=False,
    )
```

```python
import jax
import jax.numpy as jnp
from jax import lax
from jax.experimental import pallas as pl
from jax.experimental.pallas import tpu as pltpu
from jax.sharding import PartitionSpec as P

F32 = jnp.float32
BF16 = jnp.bfloat16
MESH = pl.DeviceIdType.MESH

N_XZ, C_RS, A_AG, D_RS, D_AG = range(0, 10, 2)
F_RS, F_AG, L_XZ, L_C, U_AG, Y_RS, Y_AG, X_RS, X_C, S_X, O_AG, O_X = range(10, 22)
TRANSFERS = 22
HALVES = (0, 1)
FAR_FIRST = (4, 3, 5, 2, 6, 1, 7)


def swap_halves(v):
    flat = v.reshape(-1, 128)
    return pltpu.roll(flat, 64, 1).reshape(v.shape)


def left_half(shape):
    return lax.broadcasted_iota(jnp.int32, shape, len(shape) - 1) < 64


def pack_quarters(top, bottom):
    left = left_half(top.shape)
    return jnp.where(left, top, swap_halves(bottom)), jnp.where(left, swap_halves(top), bottom)


def kernel(
    child_h, rhs_h, link_h, root_h, root_rhs_h, structure_h,
    child_out_h, root_out_h,
    raw, child, rhs, link, root, root_rhs, child_t, link_t, root_t,
    f_send, f_recv, f_mine, f_all, l_send, l_recv, lx_all, c_send, c_recv,
    u_all, spread, y_send, y_recv, y_all, x_send, x_recv, x_all, n_send, n_recv, n_all,
    c2_send, c2_recv, a_all, d_send, d_recv, d_all, o_all, o_recv, root_out,
    ids_v, ids, local_sem, send_sem, recv_sem,
):
    leaf, row, col = (lax.axis_index(a) for a in ("leaf", "row", "col"))
    place = {"leaf": leaf, "row": row, "col": col}
    size = {"leaf": 4, "row": 8, "col": 8}
    sends = []

    def peer(axis, step):
        return lax.rem(place[axis] + step, size[axis])

    def copy(number, arrival, source, target, device):
        return pltpu.make_async_remote_copy(
            src_ref=source, dst_ref=target,
            send_sem=send_sem.at[number], recv_sem=recv_sem.at[arrival],
            device_id=device, device_id_type=MESH,
        )

    def start(number, axis, source, target, whole):
        for step in FAR_FIRST if size[axis] == 8 else (2, 1, 3):
            there = peer(axis, step)
            copy(number, number, source(there), target(step), {axis: there}).start()
        pending = copy(number, number, whole, whole, {axis: peer(axis, 1)})
        sends.append(pending)
        return pending

    def scatter(number, axis, parts, landing):
        return start(
            number, axis, lambda there: parts.at[there], lambda step: landing.at[step], parts.at[pl.ds(0, size[axis] - 1)]
        )

    def gather(number, axis, whole):
        mine = whole.at[place[axis]]
        return start(number, axis, lambda there: mine, lambda step: mine, whole.at[pl.ds(0, size[axis] - 1)])

    def arrived(pending):
        pending.wait_recv()

    def total(axis, parts, landing):
        value = parts[place[axis]].astype(F32)
        for step in range(1, size[axis]):
            value = value + landing[step].astype(F32)
        return value

    def dot(a, b):
        return jnp.dot(a, b, preferred_element_type=F32)

    loads = [
        pltpu.make_async_copy(src, dst, local_sem.at[n])
        for n, (src, dst) in enumerate(
            (
                (structure_h, ids_v.at[leaf]), (child_h, raw), (rhs_h, rhs), (link_h, link), (root_rhs_h, root_rhs), (root_h, root),
            )
        )
    ]
    for n in (1, 2, 0):
        loads[n].start()
    barrier = pltpu.get_barrier_semaphore()
    for step in range(1, 8):
        pl.semaphore_signal(barrier, inc=1, device_id={"col": peer("col", step)}, device_id_type=MESH)
    for step in range(1, 32):
        there = {"leaf": peer("leaf", step // 8), "row": peer("row", step % 8)}
        pl.semaphore_signal(barrier, inc=1, device_id=there, device_id_type=MESH)

    loads[1].wait()
    for a in range(2):
        for x in range(2):
            child[a, x] = raw[a, :, x, :]
    loads[2].wait()
    for a in range(2):
        part = dot(child[a, 0], rhs[0]) + dot(child[a, 1], rhs[1])
        f_send[pl.ds(4 * a, 4)] = part.reshape(4, 64, 256).astype(BF16)
    pl.semaphore_wait(barrier, 38)
    pending = scatter(F_RS, "col", f_send, f_recv)
    for load in loads[3:]:
        load.start()
    loads[0].wait()
    mine = ids_v.at[leaf]
    structure_pending = start(
        S_X, "leaf", lambda there: structure_h, lambda step: ids_v.at[leaf], ids_v.at[pl.ds(0, 3)]
    )
    loads[3].wait()
    for a in range(2):
        for m in range(3):
            link_t[m, a] = link[a, m].T
    arrived(pending)
    f_mine[...] = total("col", f_send, f_recv)
    f_all[col] = f_mine[...].astype(BF16)
    pending = gather(F_AG, "col", f_all)
    for a in range(2):
        for x in range(2):
            child_t[x, a] = child[a, x].T
    arrived(pending)

    near, side = leaf // 2, lax.rem(leaf, 2)
    for h in (1 - near, near):
        lanes = pl.ds(pl.multiple_of(128 * h, 128), 128)
        for m in range(3):
            part = jnp.zeros((256, 128), F32)
            for a in range(2):
                part = part + dot(link_t[m, a], f_all[pl.ds(4 * a, 4), :, lanes].reshape(256, 128))
            part = part.reshape(8, 2, 16, 128)
            for q, packed in enumerate(pack_quarters(part[:, 0], part[:, 1])):
                l_send[2 * h + q, :, m] = packed.astype(BF16)
        for n, there in enumerate((2 * h + side, 2 * h + 1 - side) if h is not near else (2 * h + 1 - side, leaf)):
            for step in FAR_FIRST + (() if h is near and n else (0,)):
                at = peer("row", step)
                copy(L_XZ, L_XZ, l_send.at[there, at], l_recv.at[leaf * 8 + step], {"leaf": there, "row": at}).start()
    pltpu.make_async_copy(l_send.at[leaf, row], l_recv.at[leaf * 8], recv_sem.at[L_XZ]).start()
    pending = copy(L_XZ, L_XZ, l_recv.at[pl.ds(0, 31)], l_recv, {"row": peer("row", 1)})
    sends.append(pending)
    loads[4].wait()
    loads[5].wait()

    def turn(n, carry):
        a, x = n // 6, n % 6
        root_t[x * 6 + a] = root[a * 6 + x].T
        return carry

    lax.fori_loop(0, 12, turn, 0)
    arrived(structure_pending)
    to_scalars = pltpu.make_async_copy(ids_v, ids, local_sem.at[8])
    to_scalars.start()
    to_scalars.wait()
    arrived(pending)
    for child_at in range(4):
        value = l_recv[child_at * 8].astype(F32)
        for step in range(1, 8):
            value = value + l_recv[child_at * 8 + step].astype(F32)
        lx_all[child_at] = value

    block = lax.broadcasted_iota(jnp.int32, (6, 16, 128), 0) * 8
    for target in range(8):
        value = jnp.zeros((6, 16, 128), F32)
        for child_at in range(4):
            for m in range(3):
                wanted = ids[child_at, 0, col + 8 * m] - target
                value = value + jnp.where(block == wanted, lx_all[child_at, m][None], 0.0)
        c_send[target] = value.astype(BF16)
    pending = scatter(L_C, "col", c_send, c_recv)
    base = root_rhs[:, pl.ds(pl.multiple_of(row * 32, 32), 32), pl.ds(pl.multiple_of((leaf // 2) * 128, 128), 128)]
    base = base.astype(F32)
    first, second = pack_quarters(base[:, :16], base[:, 16:])
    base = jnp.where(leaf % 2 == 0, first, second)
    arrived(pending)
    u_all[row] = (base - total("col", c_send, c_recv)).astype(BF16)
    pending = gather(U_AG, "row", u_all)
    lax.fori_loop(12, 36, turn, 0)
    left = left_half((8, 16, 128))
    keep_left = jnp.where(left, 1.0, 0.0).astype(BF16)
    keep_right = jnp.where(left, 0.0, 1.0).astype(BF16)

    def spread_out(whole):
        for a in range(6):
            spread[a, :, 0] = whole[:, a] * keep_left
            spread[a, :, 1] = whole[:, a] * keep_right

    def root_product(matrix, parts):
        for a in range(6):
            value = jnp.zeros((256, 128), F32)
            for x in range(6):
                value = value + dot(matrix[a * 6 + x], spread[x].reshape(256, 128))
            value = value + swap_halves(value)
            value = value.reshape(8, 2, 16, 128)
            parts[:, a] = jnp.where(left, value[:, 0], value[:, 1]).astype(BF16)

    arrived(pending)
    spread_out(u_all)
    root_product(root, y_send)
    pending = scatter(Y_RS, "col", y_send, y_recv)
    arrived(pending)
    y_all[col] = total("col", y_send, y_recv).astype(BF16)
    pending = gather(Y_AG, "col", y_all)
    arrived(pending)
    spread_out(y_all)
    root_product(root_t, x_send)
    pending = scatter(X_RS, "row", x_send, x_recv)
    arrived(pending)
    solved = total("row", x_send, x_recv).astype(BF16)
    x_all[col] = solved
    pending = gather(X_C, "col", x_all)
    o_all[row] = solved
    out_pending = gather(O_AG, "row", o_all)
    arrived(pending)

    for child_at in range(4):
        for m in range(3):
            r = ids[child_at, 0, col + 8 * m]
            n_send[child_at, m] = x_all[r & 7, r >> 3]
    half_at = N_XZ + leaf // 2
    for step in FAR_FIRST + (0,):
        for leaf_step in (0, 1, 2, 3) if step else (1, 2, 3):
            there, at = peer("leaf", leaf_step), peer("row", step)
            copy(N_XZ, half_at, n_send.at[there], n_recv.at[leaf, row], {"leaf": there, "row": at}).start()
    pltpu.make_async_copy(n_send.at[leaf], n_recv.at[leaf, row], recv_sem.at[half_at]).start()
    sends.append(copy(N_XZ, N_XZ, l_recv.at[pl.ds(0, 31)], l_recv, {"row": peer("row", 1)}))

    def unpack(even, odd):
        even, odd = even.astype(F32), odd.astype(F32)
        mask = left_half(even.shape)
        top = jnp.where(mask, even, swap_halves(odd))
        bottom = jnp.where(mask, swap_halves(even), odd)
        return top.astype(BF16), bottom.astype(BF16)

    flight = {}
    for h in HALVES:
        pieces = n_recv.at[pl.ds(2 * h, 2)]
        arrived(copy(N_XZ, N_XZ + h, pieces, pieces, {"row": peer("row", 1)}))
        for m in range(3):
            n_all[m, :, 0], n_all[m, :, 1] = unpack(n_recv[2 * h, :, m], n_recv[2 * h + 1, :, m])
        for a in range(2):
            part = jnp.zeros((256, 128), F32)
            for m in range(3):
                part = part + dot(link[a, m], n_all[m].reshape(256, 128))
            c2_send[h, pl.ds(4 * a, 4)] = part.reshape(4, 64, 128).astype(BF16)
        flight[h] = scatter(C_RS + h, "col", c2_send.at[h], c2_recv.at[h])
    arrived(out_pending)
    o_recv[leaf] = o_all[...]
    out_pending = start(O_X, "leaf", lambda there: o_all, lambda step: o_recv.at[leaf], o_recv.at[pl.ds(0, 3)])
    for h in HALVES:
        arrived(flight[h])
        carried = total("col", c2_send.at[h], c2_recv.at[h])
        a_all[h, col] = (f_mine[:, pl.ds(128 * h, 128)] - carried).astype(BF16)
        flight[h] = gather(A_AG + h, "col", a_all.at[h])

    for h in HALVES:
        arrived(flight[h])
        for x in range(2):
            part = jnp.zeros((256, 128), F32)
            for a in range(2):
                part = part + dot(child_t[x, a], a_all[h, pl.ds(4 * a, 4)].reshape(256, 128))
            d_send[h, pl.ds(4 * x, 4)] = part.reshape(4, 64, 128).astype(BF16)
        flight[h] = scatter(D_RS + h, "row", d_send.at[h], d_recv.at[h])
    for h in HALVES:
        arrived(flight[h])
        d_all[h, row] = total("row", d_send.at[h], d_recv.at[h]).astype(BF16)
        flight[h] = gather(D_AG + h, "row", d_all.at[h])
    arrived(out_pending)
    for h in HALVES:
        for r in range(8):
            top, bottom = unpack(o_recv[2 * h, r], o_recv[2 * h + 1, r])
            root_out[:, pl.ds(32 * r, 16), pl.ds(128 * h, 128)] = top
            root_out[:, pl.ds(32 * r + 16, 16), pl.ds(128 * h, 128)] = bottom
    stores = [pltpu.make_async_copy(root_out, root_out_h, local_sem.at[9])]
    stores[0].start()
    for h in HALVES:
        arrived(flight[h])
        store = pltpu.make_async_copy(d_all.at[h], child_out_h.at[:, :, pl.ds(128 * h, 128)], local_sem.at[10 + h])
        store.start()
        stores.append(store)
    for store in stores:
        store.wait()
    for pending in sends:
        pending.wait_send()


def on_device(child_rhs, child_inv, root_inv, coupling, root_rhs, structure):
    child = child_inv[0, :, 0, :, :, 0, :]
    rhs = child_rhs[0, :, 0]
    link = coupling[0, :, 0, :, :, 0, :].transpose(0, 2, 1, 3)
    root = root_inv[:, 0, :, :, 0, :].transpose(0, 2, 1, 3).reshape(36, 256, 256)
    away = pl.BlockSpec(memory_space=pltpu.HBM)
    packed = (6, 16, 128)
    half = (2, 8, 64, 128)
    shapes = [
        (2, 256, 2, 256), (2, 2, 256, 256), (2, 256, 256), (2, 3, 256, 256), (36, 256, 256), (6, 256, 256),
        (2, 2, 256, 256), (3, 2, 256, 256), (36, 256, 256),
        (8, 64, 256), (8, 64, 256), None, (8, 64, 256),
        (4, 8, 3, 16, 128), (32, 3, 16, 128), None, (8,) + packed, (8,) + packed,
        (8,) + packed, (6, 8, 2, 16, 128),
        (8,) + packed, (8,) + packed, (8,) + packed,
        (8,) + packed, (8,) + packed, (8,) + packed,
        (4, 3, 16, 128), (4, 8, 3, 16, 128), (3, 8, 2, 16, 128),
        half, half, half,
        half, half, half,
        (8,) + packed, (4, 8) + packed, (6, 256, 256),
    ]
    wide = iter([(64, 256), (4, 3, 16, 128)])
    scratch = [
        pltpu.VMEM(next(wide), F32) if shape is None else pltpu.VMEM(shape, BF16) for shape in shapes
    ]
    scratch += [
        pltpu.VMEM((4, 1, 24), jnp.int32),
        pltpu.SMEM((4, 1, 24), jnp.int32),
        pltpu.SemaphoreType.DMA((12,)),
        pltpu.SemaphoreType.DMA((TRANSFERS,)),
        pltpu.SemaphoreType.DMA((TRANSFERS,)),
    ]
    child_x, root_x = pl.pallas_call(
        kernel,
        out_shape=(
            jax.ShapeDtypeStruct((8, 64, 256), BF16),
            jax.ShapeDtypeStruct((6, 256, 256), BF16),
        ),
        in_specs=[away] * 6,
        out_specs=(away, away),
        scratch_shapes=scratch,
        compiler_params=pltpu.CompilerParams(
            collective_id=0, has_side_effects=True, vmem_limit_bytes=60 * 1024 * 1024
        ),
        cost_estimate=pl.CostEstimate(flops=3_000_000_000, bytes_accessed=10_000_000, transcendentals=0),
        name="substitution",
    )(child, rhs, link, root, root_rhs[:, 0], structure)
    child_x = child_x.reshape(2, 256, 256).astype(F32)
    return child_x[None, :, None], root_x.astype(F32)[:, None]


def solution(mesh):
    placed = (
        P("leaf", None, "col", None, None),
        P("leaf", None, "row", None, None, "col", None),
        P(None, "row", None, None, "col", None),
        P("leaf", None, "row", None, None, "col", None),
        P(None, "col", None, None),
        P("leaf", None),
    )
    return jax.shard_map(
        on_device,
        mesh=mesh,
        in_specs=placed,
        out_specs=(P("leaf", None, "col", None, None), P(None, "col", None, None)),
        check_vma=False,
    )
```

```python
import jax
import jax.numpy as jnp
from jax import lax
from jax.experimental import pallas as pl
from jax.experimental.pallas import tpu as pltpu
from jax.sharding import PartitionSpec as P

F32 = jnp.float32
BF16 = jnp.bfloat16
MESH = pl.DeviceIdType.MESH

N_XZ, C_RS, A_AG, D_RS, D_AG = range(0, 10, 2)
F_RS, F_AG, L_XZ, L_C, U_AG, Y_RS, Y_AG, X_RS, X_C, S_X, O_AG, O_X = range(10, 22)
TRANSFERS = 22
HALVES = (0, 1)
FAR_FIRST = (4, 3, 5, 2, 6, 1, 7)


def swap_halves(v):
    flat = v.reshape(-1, 128)
    return pltpu.roll(flat, 64, 1).reshape(v.shape)


def left_half(shape):
    return lax.broadcasted_iota(jnp.int32, shape, len(shape) - 1) < 64


def pack_quarters(top, bottom):
    left = left_half(top.shape)
    return jnp.where(left, top, swap_halves(bottom)), jnp.where(left, swap_halves(top), bottom)


def kernel(
    child_h, rhs_h, link_h, root_h, root_rhs_h, structure_h,
    child_out_h, root_out_h,
    raw, child, rhs, link, root, root_rhs, child_t, link_t, root_t,
    f_send, f_recv, f_mine, f_all, l_send, l_recv, lx_all, c_send, c_recv,
    u_all, spread, y_send, y_recv, y_all, x_send, x_recv, x_all, n_send, n_recv, n_all,
    c2_send, c2_recv, a_all, d_send, d_recv, d_all, o_all, o_recv, root_out,
    ids_v, ids, local_sem, send_sem, recv_sem,
):
    leaf, row, col = (lax.axis_index(a) for a in ("leaf", "row", "col"))
    place = {"leaf": leaf, "row": row, "col": col}
    size = {"leaf": 4, "row": 8, "col": 8}
    sends = []

    def peer(axis, step):
        return lax.rem(place[axis] + step, size[axis])

    def copy(number, arrival, source, target, device):
        return pltpu.make_async_remote_copy(
            src_ref=source, dst_ref=target,
            send_sem=send_sem.at[number], recv_sem=recv_sem.at[arrival],
            device_id=device, device_id_type=MESH,
        )

    def start(number, axis, source, target, whole):
        for step in FAR_FIRST if size[axis] == 8 else (2, 1, 3):
            there = peer(axis, step)
            copy(number, number, source(there), target(step), {axis: there}).start()
        pending = copy(number, number, whole, whole, {axis: peer(axis, 1)})
        sends.append(pending)
        return pending

    def scatter(number, axis, parts, landing):
        return start(
            number, axis, lambda there: parts.at[there], lambda step: landing.at[step], parts.at[pl.ds(0, size[axis] - 1)]
        )

    def gather(number, axis, whole):
        mine = whole.at[place[axis]]
        return start(number, axis, lambda there: mine, lambda step: mine, whole.at[pl.ds(0, size[axis] - 1)])

    def arrived(pending):
        pending.wait_recv()

    def total(axis, parts, landing):
        value = parts[place[axis]].astype(F32)
        for step in range(1, size[axis]):
            value = value + landing[step].astype(F32)
        return value

    def dot(a, b):
        return jnp.dot(a, b, preferred_element_type=F32)

    loads = [
        pltpu.make_async_copy(src, dst, local_sem.at[n])
        for n, (src, dst) in enumerate(
            (
                (structure_h, ids_v.at[leaf]), (child_h, raw), (rhs_h, rhs), (link_h, link), (root_rhs_h, root_rhs), (root_h, root),
            )
        )
    ]
    for n in (1, 2, 0):
        loads[n].start()
    barrier = pltpu.get_barrier_semaphore()
    for step in range(1, 8):
        pl.semaphore_signal(barrier, inc=1, device_id={"col": peer("col", step)}, device_id_type=MESH)
    for step in range(1, 32):
        there = {"leaf": peer("leaf", step // 8), "row": peer("row", step % 8)}
        pl.semaphore_signal(barrier, inc=1, device_id=there, device_id_type=MESH)

    loads[1].wait()
    for a in range(2):
        for x in range(2):
            child[a, x] = raw[a, :, x, :]
    loads[2].wait()
    for a in range(2):
        part = dot(child[a, 0], rhs[0]) + dot(child[a, 1], rhs[1])
        f_send[pl.ds(4 * a, 4)] = part.reshape(4, 64, 256).astype(BF16)
    pl.semaphore_wait(barrier, 38)
    pending = scatter(F_RS, "col", f_send, f_recv)
    for load in loads[3:]:
        load.start()
    loads[0].wait()
    mine = ids_v.at[leaf]
    structure_pending = start(
        S_X, "leaf", lambda there: structure_h, lambda step: ids_v.at[leaf], ids_v.at[pl.ds(0, 3)]
    )
    loads[3].wait()
    for a in range(2):
        for m in range(3):
            link_t[m, a] = link[a, m].T
    arrived(pending)
    f_mine[...] = total("col", f_send, f_recv)
    f_all[col] = f_mine[...].astype(BF16)
    pending = gather(F_AG, "col", f_all)
    for a in range(2):
        for x in range(2):
            child_t[x, a] = child[a, x].T
    arrived(pending)

    for h in HALVES:
        for m in range(3):
            part = jnp.zeros((256, 128), F32)
            for a in range(2):
                part = part + dot(link_t[m, a], f_all[pl.ds(4 * a, 4), :, pl.ds(128 * h, 128)].reshape(256, 128))
            part = part.reshape(8, 2, 16, 128)
            for q, packed in enumerate(pack_quarters(part[:, 0], part[:, 1])):
                l_send[2 * h + q, :, m] = packed.astype(BF16)
        for step in FAR_FIRST:
            for there in (2 * h, 2 * h + 1):
                at = peer("row", step)
                copy(L_XZ, L_XZ, l_send.at[there, at], l_recv.at[leaf * 8 + step], {"leaf": there, "row": at}).start()
    for step in (2, 1, 3):
        there = peer("leaf", step)
        copy(L_XZ, L_XZ, l_send.at[there, row], l_recv.at[leaf * 8], {"leaf": there}).start()
    pltpu.make_async_copy(l_send.at[leaf, row], l_recv.at[leaf * 8], recv_sem.at[L_XZ]).start()
    pending = copy(L_XZ, L_XZ, l_recv.at[pl.ds(0, 31)], l_recv, {"row": peer("row", 1)})
    sends.append(pending)
    loads[4].wait()
    loads[5].wait()

    def turn(n, carry):
        a, x = n // 6, n % 6
        root_t[x * 6 + a] = root[a * 6 + x].T
        return carry

    lax.fori_loop(0, 12, turn, 0)
    arrived(structure_pending)
    to_scalars = pltpu.make_async_copy(ids_v, ids, local_sem.at[8])
    to_scalars.start()
    to_scalars.wait()
    arrived(pending)
    for child_at in range(4):
        value = l_recv[child_at * 8].astype(F32)
        for step in range(1, 8):
            value = value + l_recv[child_at * 8 + step].astype(F32)
        lx_all[child_at] = value

    block = lax.broadcasted_iota(jnp.int32, (6, 16, 128), 0) * 8
    for target in range(8):
        value = jnp.zeros((6, 16, 128), F32)
        for child_at in range(4):
            for m in range(3):
                wanted = ids[child_at, 0, col + 8 * m] - target
                value = value + jnp.where(block == wanted, lx_all[child_at, m][None], 0.0)
        c_send[target] = value.astype(BF16)
    pending = scatter(L_C, "col", c_send, c_recv)
    base = root_rhs[:, pl.ds(pl.multiple_of(row * 32, 32), 32), pl.ds(pl.multiple_of((leaf // 2) * 128, 128), 128)]
    base = base.astype(F32)
    first, second = pack_quarters(base[:, :16], base[:, 16:])
    base = jnp.where(leaf % 2 == 0, first, second)
    arrived(pending)
    u_all[row] = (base - total("col", c_send, c_recv)).astype(BF16)
    pending = gather(U_AG, "row", u_all)
    lax.fori_loop(12, 36, turn, 0)
    left = left_half((8, 16, 128))
    keep_left = jnp.where(left, 1.0, 0.0).astype(BF16)
    keep_right = jnp.where(left, 0.0, 1.0).astype(BF16)

    def spread_out(whole):
        for a in range(6):
            spread[a, :, 0] = whole[:, a] * keep_left
            spread[a, :, 1] = whole[:, a] * keep_right

    def root_product(matrix, parts):
        for a in range(6):
            value = jnp.zeros((256, 128), F32)
            for x in range(6):
                value = value + dot(matrix[a * 6 + x], spread[x].reshape(256, 128))
            value = value + swap_halves(value)
            value = value.reshape(8, 2, 16, 128)
            parts[:, a] = jnp.where(left, value[:, 0], value[:, 1]).astype(BF16)

    arrived(pending)
    spread_out(u_all)
    root_product(root, y_send)
    pending = scatter(Y_RS, "col", y_send, y_recv)
    arrived(pending)
    y_all[col] = total("col", y_send, y_recv).astype(BF16)
    pending = gather(Y_AG, "col", y_all)
    arrived(pending)
    spread_out(y_all)
    root_product(root_t, x_send)
    pending = scatter(X_RS, "row", x_send, x_recv)
    arrived(pending)
    solved = total("row", x_send, x_recv).astype(BF16)
    x_all[col] = solved
    pending = gather(X_C, "col", x_all)
    o_all[row] = solved
    arrived(pending)

    for child_at in range(4):
        for m in range(3):
            r = ids[child_at, 0, col + 8 * m]
            n_send[child_at, m] = x_all[r & 7, r >> 3]
    half_at = N_XZ + leaf // 2
    for step in FAR_FIRST + (0,):
        for leaf_step in (0, 1, 2, 3) if step else (1, 2, 3):
            there, at = peer("leaf", leaf_step), peer("row", step)
            copy(N_XZ, half_at, n_send.at[there], n_recv.at[leaf, row], {"leaf": there, "row": at}).start()
    pltpu.make_async_copy(n_send.at[leaf], n_recv.at[leaf, row], recv_sem.at[half_at]).start()
    sends.append(copy(N_XZ, N_XZ, l_recv.at[pl.ds(0, 31)], l_recv, {"row": peer("row", 1)}))

    def unpack(even, odd):
        even, odd = even.astype(F32), odd.astype(F32)
        mask = left_half(even.shape)
        top = jnp.where(mask, even, swap_halves(odd))
        bottom = jnp.where(mask, swap_halves(even), odd)
        return top.astype(BF16), bottom.astype(BF16)

    flight = {}
    for h in HALVES:
        pieces = n_recv.at[pl.ds(2 * h, 2)]
        arrived(copy(N_XZ, N_XZ + h, pieces, pieces, {"row": peer("row", 1)}))
        for m in range(3):
            n_all[m, :, 0], n_all[m, :, 1] = unpack(n_recv[2 * h, :, m], n_recv[2 * h + 1, :, m])
        for a in range(2):
            part = jnp.zeros((256, 128), F32)
            for m in range(3):
                part = part + dot(link[a, m], n_all[m].reshape(256, 128))
            c2_send[h, pl.ds(4 * a, 4)] = part.reshape(4, 64, 128).astype(BF16)
        flight[h] = scatter(C_RS + h, "col", c2_send.at[h], c2_recv.at[h])
    out_pending = gather(O_AG, "row", o_all)
    for h in HALVES:
        arrived(flight[h])
        carried = total("col", c2_send.at[h], c2_recv.at[h])
        a_all[h, col] = (f_mine[:, pl.ds(128 * h, 128)] - carried).astype(BF16)
        flight[h] = gather(A_AG + h, "col", a_all.at[h])

    for h in HALVES:
        arrived(flight[h])
        for x in range(2):
            part = jnp.zeros((256, 128), F32)
            for a in range(2):
                part = part + dot(child_t[x, a], a_all[h, pl.ds(4 * a, 4)].reshape(256, 128))
            d_send[h, pl.ds(4 * x, 4)] = part.reshape(4, 64, 128).astype(BF16)
        flight[h] = scatter(D_RS + h, "row", d_send.at[h], d_recv.at[h])
    arrived(out_pending)
    o_recv[leaf] = o_all[...]
    out_pending = start(O_X, "leaf", lambda there: o_all, lambda step: o_recv.at[leaf], o_recv.at[pl.ds(0, 3)])
    for h in HALVES:
        arrived(flight[h])
        d_all[h, row] = total("row", d_send.at[h], d_recv.at[h]).astype(BF16)
        flight[h] = gather(D_AG + h, "row", d_all.at[h])
    arrived(out_pending)
    for h in HALVES:
        for r in range(8):
            top, bottom = unpack(o_recv[2 * h, r], o_recv[2 * h + 1, r])
            root_out[:, pl.ds(32 * r, 16), pl.ds(128 * h, 128)] = top
            root_out[:, pl.ds(32 * r + 16, 16), pl.ds(128 * h, 128)] = bottom
    stores = [pltpu.make_async_copy(root_out, root_out_h, local_sem.at[9])]
    stores[0].start()
    for h in HALVES:
        arrived(flight[h])
        store = pltpu.make_async_copy(d_all.at[h], child_out_h.at[:, :, pl.ds(128 * h, 128)], local_sem.at[10 + h])
        store.start()
        stores.append(store)
    for store in stores:
        store.wait()
    for pending in sends:
        pending.wait_send()


def on_device(child_rhs, child_inv, root_inv, coupling, root_rhs, structure):
    child = child_inv[0, :, 0, :, :, 0, :]
    rhs = child_rhs[0, :, 0]
    link = coupling[0, :, 0, :, :, 0, :].transpose(0, 2, 1, 3)
    root = root_inv[:, 0, :, :, 0, :].transpose(0, 2, 1, 3).reshape(36, 256, 256)
    away = pl.BlockSpec(memory_space=pltpu.HBM)
    packed = (6, 16, 128)
    half = (2, 8, 64, 128)
    shapes = [
        (2, 256, 2, 256), (2, 2, 256, 256), (2, 256, 256), (2, 3, 256, 256), (36, 256, 256), (6, 256, 256),
        (2, 2, 256, 256), (3, 2, 256, 256), (36, 256, 256),
        (8, 64, 256), (8, 64, 256), None, (8, 64, 256),
        (4, 8, 3, 16, 128), (32, 3, 16, 128), None, (8,) + packed, (8,) + packed,
        (8,) + packed, (6, 8, 2, 16, 128),
        (8,) + packed, (8,) + packed, (8,) + packed,
        (8,) + packed, (8,) + packed, (8,) + packed,
        (4, 3, 16, 128), (4, 8, 3, 16, 128), (3, 8, 2, 16, 128),
        half, half, half,
        half, half, half,
        (8,) + packed, (4, 8) + packed, (6, 256, 256),
    ]
    wide = iter([(64, 256), (4, 3, 16, 128)])
    scratch = [
        pltpu.VMEM(next(wide), F32) if shape is None else pltpu.VMEM(shape, BF16) for shape in shapes
    ]
    scratch += [
        pltpu.VMEM((4, 1, 24), jnp.int32),
        pltpu.SMEM((4, 1, 24), jnp.int32),
        pltpu.SemaphoreType.DMA((12,)),
        pltpu.SemaphoreType.DMA((TRANSFERS,)),
        pltpu.SemaphoreType.DMA((TRANSFERS,)),
    ]
    child_x, root_x = pl.pallas_call(
        kernel,
        out_shape=(
            jax.ShapeDtypeStruct((8, 64, 256), BF16),
            jax.ShapeDtypeStruct((6, 256, 256), BF16),
        ),
        in_specs=[away] * 6,
        out_specs=(away, away),
        scratch_shapes=scratch,
        compiler_params=pltpu.CompilerParams(
            collective_id=0, has_side_effects=True, vmem_limit_bytes=60 * 1024 * 1024
        ),
        cost_estimate=pl.CostEstimate(flops=3_000_000_000, bytes_accessed=10_000_000, transcendentals=0),
        name="substitution",
    )(child, rhs, link, root, root_rhs[:, 0], structure)
    child_x = child_x.reshape(2, 256, 256).astype(F32)
    return child_x[None, :, None], root_x.astype(F32)[:, None]


def solution(mesh):
    placed = (
        P("leaf", None, "col", None, None),
        P("leaf", None, "row", None, None, "col", None),
        P(None, "row", None, None, "col", None),
        P("leaf", None, "row", None, None, "col", None),
        P(None, "col", None, None),
        P("leaf", None),
    )
    return jax.shard_map(
        on_device,
        mesh=mesh,
        in_specs=placed,
        out_specs=(P("leaf", None, "col", None, None), P(None, "col", None, None)),
        check_vma=False,
    )
```

```python
import jax
import jax.numpy as jnp
from jax import lax
from jax.experimental import pallas as pl
from jax.experimental.pallas import tpu as pltpu
from jax.sharding import PartitionSpec as P

F32 = jnp.float32
BF16 = jnp.bfloat16
MESH = pl.DeviceIdType.MESH

N_XZ, C_RS, A_AG, D_RS, D_AG = range(0, 10, 2)
F_RS, F_AG, L_XZ, L_C, U_AG, Y_RS, Y_AG, X_RS, X_C, S_X, O_AG, O_X, X_RS2 = range(10, 23)
TRANSFERS = 23
HALVES = (0, 1)
FAR_FIRST = (4, 3, 5, 2, 6, 1, 7)


def swap_halves(v):
    flat = v.reshape(-1, 128)
    return pltpu.roll(flat, 64, 1).reshape(v.shape)


def left_half(shape):
    return lax.broadcasted_iota(jnp.int32, shape, len(shape) - 1) < 64


def pack_quarters(top, bottom):
    left = left_half(top.shape)
    return jnp.where(left, top, swap_halves(bottom)), jnp.where(left, swap_halves(top), bottom)


def kernel(
    child_h, rhs_h, link_h, root_h, root_rhs_h, structure_h,
    child_out_h, root_out_h,
    raw, child, rhs, link, root, root_rhs, child_t, link_t, root_t,
    f_send, f_recv, f_mine, f_all, l_send, l_recv, lx_all, c_send, c_recv,
    u_all, spread, y_send, y_recv, y_all, x_send, x_recv, x_all, n_send, n_recv, n_all,
    c2_send, c2_recv, a_all, d_send, d_recv, d_all, o_all, o_recv, root_out,
    ids_v, ids, local_sem, send_sem, recv_sem,
):
    leaf, row, col = (lax.axis_index(a) for a in ("leaf", "row", "col"))
    place = {"leaf": leaf, "row": row, "col": col}
    size = {"leaf": 4, "row": 8, "col": 8}
    sends = []

    def peer(axis, step):
        return lax.rem(place[axis] + step, size[axis])

    def copy(number, arrival, source, target, device):
        return pltpu.make_async_remote_copy(
            src_ref=source, dst_ref=target,
            send_sem=send_sem.at[number], recv_sem=recv_sem.at[arrival],
            device_id=device, device_id_type=MESH,
        )

    def start(number, axis, source, target, whole):
        for step in FAR_FIRST if size[axis] == 8 else (2, 1, 3):
            there = peer(axis, step)
            copy(number, number, source(there), target(step), {axis: there}).start()
        pending = copy(number, number, whole, whole, {axis: peer(axis, 1)})
        sends.append(pending)
        return pending

    def scatter(number, axis, parts, landing):
        return start(
            number, axis, lambda there: parts.at[there], lambda step: landing.at[step], parts.at[pl.ds(0, size[axis] - 1)]
        )

    def gather(number, axis, whole):
        mine = whole.at[place[axis]]
        return start(number, axis, lambda there: mine, lambda step: mine, whole.at[pl.ds(0, size[axis] - 1)])

    def arrived(pending):
        pending.wait_recv()

    def total(axis, parts, landing):
        value = parts[place[axis]].astype(F32)
        for step in range(1, size[axis]):
            value = value + landing[step].astype(F32)
        return value

    def dot(a, b):
        return jnp.dot(a, b, preferred_element_type=F32)

    loads = [
        pltpu.make_async_copy(src, dst, local_sem.at[n])
        for n, (src, dst) in enumerate(
            (
                (structure_h, ids_v.at[leaf]), (child_h, raw), (rhs_h, rhs), (link_h, link), (root_rhs_h, root_rhs), (root_h, root),
            )
        )
    ]
    for n in (1, 2, 0):
        loads[n].start()
    barrier = pltpu.get_barrier_semaphore()
    for step in range(1, 8):
        pl.semaphore_signal(barrier, inc=1, device_id={"col": peer("col", step)}, device_id_type=MESH)
    for step in range(1, 32):
        there = {"leaf": peer("leaf", step // 8), "row": peer("row", step % 8)}
        pl.semaphore_signal(barrier, inc=1, device_id=there, device_id_type=MESH)

    loads[1].wait()
    for a in range(2):
        for x in range(2):
            child[a, x] = raw[a, :, x, :]
    loads[2].wait()
    for a in range(2):
        part = dot(child[a, 0], rhs[0]) + dot(child[a, 1], rhs[1])
        f_send[pl.ds(4 * a, 4)] = part.reshape(4, 64, 256).astype(BF16)
    pl.semaphore_wait(barrier, 38)
    pending = scatter(F_RS, "col", f_send, f_recv)
    for load in loads[3:]:
        load.start()
    loads[0].wait()
    mine = ids_v.at[leaf]
    structure_pending = start(
        S_X, "leaf", lambda there: structure_h, lambda step: ids_v.at[leaf], ids_v.at[pl.ds(0, 3)]
    )
    loads[3].wait()
    for a in range(2):
        for m in range(3):
            link_t[m, a] = link[a, m].T
    arrived(pending)
    f_mine[...] = total("col", f_send, f_recv)
    f_all[col] = f_mine[...].astype(BF16)
    pending = gather(F_AG, "col", f_all)
    for a in range(2):
        for x in range(2):
            child_t[x, a] = child[a, x].T
    arrived(pending)

    for h in HALVES:
        for m in range(3):
            part = jnp.zeros((256, 128), F32)
            for a in range(2):
                part = part + dot(link_t[m, a], f_all[pl.ds(4 * a, 4), :, pl.ds(128 * h, 128)].reshape(256, 128))
            part = part.reshape(8, 2, 16, 128)
            for q, packed in enumerate(pack_quarters(part[:, 0], part[:, 1])):
                l_send[2 * h + q, :, m] = packed.astype(BF16)
        for step in FAR_FIRST:
            for there in (2 * h, 2 * h + 1):
                at = peer("row", step)
                copy(L_XZ, L_XZ, l_send.at[there, at], l_recv.at[leaf * 8 + step], {"leaf": there, "row": at}).start()
    for step in (2, 1, 3):
        there = peer("leaf", step)
        copy(L_XZ, L_XZ, l_send.at[there, row], l_recv.at[leaf * 8], {"leaf": there}).start()
    pltpu.make_async_copy(l_send.at[leaf, row], l_recv.at[leaf * 8], recv_sem.at[L_XZ]).start()
    pending = copy(L_XZ, L_XZ, l_recv.at[pl.ds(0, 31)], l_recv, {"row": peer("row", 1)})
    sends.append(pending)
    loads[4].wait()
    loads[5].wait()

    def turn(n, carry):
        a, x = n // 6, n % 6
        root_t[x * 6 + a] = root[a * 6 + x].T
        return carry

    lax.fori_loop(0, 12, turn, 0)
    arrived(structure_pending)
    to_scalars = pltpu.make_async_copy(ids_v, ids, local_sem.at[8])
    to_scalars.start()
    to_scalars.wait()
    arrived(pending)
    for child_at in range(4):
        value = l_recv[child_at * 8].astype(F32)
        for step in range(1, 8):
            value = value + l_recv[child_at * 8 + step].astype(F32)
        lx_all[child_at] = value

    block = lax.broadcasted_iota(jnp.int32, (6, 16, 128), 0) * 8
    for target in range(8):
        value = jnp.zeros((6, 16, 128), F32)
        for child_at in range(4):
            for m in range(3):
                wanted = ids[child_at, 0, col + 8 * m] - target
                value = value + jnp.where(block == wanted, lx_all[child_at, m][None], 0.0)
        c_send[target] = value.astype(BF16)
    pending = scatter(L_C, "col", c_send, c_recv)
    base = root_rhs[:, pl.ds(pl.multiple_of(row * 32, 32), 32), pl.ds(pl.multiple_of((leaf // 2) * 128, 128), 128)]
    base = base.astype(F32)
    first, second = pack_quarters(base[:, :16], base[:, 16:])
    base = jnp.where(leaf % 2 == 0, first, second)
    arrived(pending)
    u_all[row] = (base - total("col", c_send, c_recv)).astype(BF16)
    pending = gather(U_AG, "row", u_all)
    lax.fori_loop(12, 36, turn, 0)
    left = left_half((8, 16, 128))
    keep_left = jnp.where(left, 1.0, 0.0).astype(BF16)
    keep_right = jnp.where(left, 0.0, 1.0).astype(BF16)

    def spread_out(whole):
        for a in range(6):
            spread[a, :, 0] = whole[:, a] * keep_left
            spread[a, :, 1] = whole[:, a] * keep_right

    def root_product(matrix, parts, rows=range(6)):
        for a in rows:
            value = jnp.zeros((256, 128), F32)
            for x in range(6):
                value = value + dot(matrix[a * 6 + x], spread[x].reshape(256, 128))
            value = value + swap_halves(value)
            value = value.reshape(8, 2, 16, 128)
            parts[:, a] = jnp.where(left, value[:, 0], value[:, 1]).astype(BF16)

    arrived(pending)
    spread_out(u_all)
    root_product(root, y_send)
    pending = scatter(Y_RS, "col", y_send, y_recv)
    arrived(pending)
    y_all[col] = total("col", y_send, y_recv).astype(BF16)
    pending = gather(Y_AG, "col", y_all)
    arrived(pending)
    spread_out(y_all)
    parts = []
    for number, first in ((X_RS, 0), (X_RS2, 3)):
        root_product(root_t, x_send, range(first, first + 3))
        rows = pl.ds(first, 3)
        parts.append(start(
            number, "row", lambda there: x_send.at[there, rows], lambda step: x_recv.at[step, rows],
            x_send.at[pl.ds(0, 7), rows],
        ))
    for pending in parts:
        arrived(pending)
    solved = total("row", x_send, x_recv).astype(BF16)
    x_all[col] = solved
    pending = gather(X_C, "col", x_all)
    o_all[row] = solved
    arrived(pending)

    for child_at in range(4):
        for m in range(3):
            r = ids[child_at, 0, col + 8 * m]
            n_send[child_at, m] = x_all[r & 7, r >> 3]
    half_at = N_XZ + leaf // 2
    for step in FAR_FIRST + (0,):
        for leaf_step in (0, 1, 2, 3) if step else (1, 2, 3):
            there, at = peer("leaf", leaf_step), peer("row", step)
            copy(N_XZ, half_at, n_send.at[there], n_recv.at[leaf, row], {"leaf": there, "row": at}).start()
    pltpu.make_async_copy(n_send.at[leaf], n_recv.at[leaf, row], recv_sem.at[half_at]).start()
    sends.append(copy(N_XZ, N_XZ, l_recv.at[pl.ds(0, 31)], l_recv, {"row": peer("row", 1)}))

    def unpack(even, odd):
        even, odd = even.astype(F32), odd.astype(F32)
        mask = left_half(even.shape)
        top = jnp.where(mask, even, swap_halves(odd))
        bottom = jnp.where(mask, swap_halves(even), odd)
        return top.astype(BF16), bottom.astype(BF16)

    flight = {}
    for h in HALVES:
        pieces = n_recv.at[pl.ds(2 * h, 2)]
        arrived(copy(N_XZ, N_XZ + h, pieces, pieces, {"row": peer("row", 1)}))
        for m in range(3):
            n_all[m, :, 0], n_all[m, :, 1] = unpack(n_recv[2 * h, :, m], n_recv[2 * h + 1, :, m])
        for a in range(2):
            part = jnp.zeros((256, 128), F32)
            for m in range(3):
                part = part + dot(link[a, m], n_all[m].reshape(256, 128))
            c2_send[h, pl.ds(4 * a, 4)] = part.reshape(4, 64, 128).astype(BF16)
        flight[h] = scatter(C_RS + h, "col", c2_send.at[h], c2_recv.at[h])
    out_pending = gather(O_AG, "row", o_all)
    for h in HALVES:
        arrived(flight[h])
        carried = total("col", c2_send.at[h], c2_recv.at[h])
        a_all[h, col] = (f_mine[:, pl.ds(128 * h, 128)] - carried).astype(BF16)
        flight[h] = gather(A_AG + h, "col", a_all.at[h])

    for h in HALVES:
        arrived(flight[h])
        for x in range(2):
            part = jnp.zeros((256, 128), F32)
            for a in range(2):
                part = part + dot(child_t[x, a], a_all[h, pl.ds(4 * a, 4)].reshape(256, 128))
            d_send[h, pl.ds(4 * x, 4)] = part.reshape(4, 64, 128).astype(BF16)
        flight[h] = scatter(D_RS + h, "row", d_send.at[h], d_recv.at[h])
    arrived(out_pending)
    o_recv[leaf] = o_all[...]
    out_pending = start(O_X, "leaf", lambda there: o_all, lambda step: o_recv.at[leaf], o_recv.at[pl.ds(0, 3)])
    for h in HALVES:
        arrived(flight[h])
        d_all[h, row] = total("row", d_send.at[h], d_recv.at[h]).astype(BF16)
        flight[h] = gather(D_AG + h, "row", d_all.at[h])
    arrived(out_pending)
    for h in HALVES:
        for r in range(8):
            top, bottom = unpack(o_recv[2 * h, r], o_recv[2 * h + 1, r])
            root_out[:, pl.ds(32 * r, 16), pl.ds(128 * h, 128)] = top
            root_out[:, pl.ds(32 * r + 16, 16), pl.ds(128 * h, 128)] = bottom
    stores = [pltpu.make_async_copy(root_out, root_out_h, local_sem.at[9])]
    stores[0].start()
    for h in HALVES:
        arrived(flight[h])
        store = pltpu.make_async_copy(d_all.at[h], child_out_h.at[:, :, pl.ds(128 * h, 128)], local_sem.at[10 + h])
        store.start()
        stores.append(store)
    for store in stores:
        store.wait()
    for pending in sends:
        pending.wait_send()


def on_device(child_rhs, child_inv, root_inv, coupling, root_rhs, structure):
    child = child_inv[0, :, 0, :, :, 0, :]
    rhs = child_rhs[0, :, 0]
    link = coupling[0, :, 0, :, :, 0, :].transpose(0, 2, 1, 3)
    root = root_inv[:, 0, :, :, 0, :].transpose(0, 2, 1, 3).reshape(36, 256, 256)
    away = pl.BlockSpec(memory_space=pltpu.HBM)
    packed = (6, 16, 128)
    half = (2, 8, 64, 128)
    shapes = [
        (2, 256, 2, 256), (2, 2, 256, 256), (2, 256, 256), (2, 3, 256, 256), (36, 256, 256), (6, 256, 256),
        (2, 2, 256, 256), (3, 2, 256, 256), (36, 256, 256),
        (8, 64, 256), (8, 64, 256), None, (8, 64, 256),
        (4, 8, 3, 16, 128), (32, 3, 16, 128), None, (8,) + packed, (8,) + packed,
        (8,) + packed, (6, 8, 2, 16, 128),
        (8,) + packed, (8,) + packed, (8,) + packed,
        (8,) + packed, (8,) + packed, (8,) + packed,
        (4, 3, 16, 128), (4, 8, 3, 16, 128), (3, 8, 2, 16, 128),
        half, half, half,
        half, half, half,
        (8,) + packed, (4, 8) + packed, (6, 256, 256),
    ]
    wide = iter([(64, 256), (4, 3, 16, 128)])
    scratch = [
        pltpu.VMEM(next(wide), F32) if shape is None else pltpu.VMEM(shape, BF16) for shape in shapes
    ]
    scratch += [
        pltpu.VMEM((4, 1, 24), jnp.int32),
        pltpu.SMEM((4, 1, 24), jnp.int32),
        pltpu.SemaphoreType.DMA((12,)),
        pltpu.SemaphoreType.DMA((TRANSFERS,)),
        pltpu.SemaphoreType.DMA((TRANSFERS,)),
    ]
    child_x, root_x = pl.pallas_call(
        kernel,
        out_shape=(
            jax.ShapeDtypeStruct((8, 64, 256), BF16),
            jax.ShapeDtypeStruct((6, 256, 256), BF16),
        ),
        in_specs=[away] * 6,
        out_specs=(away, away),
        scratch_shapes=scratch,
        compiler_params=pltpu.CompilerParams(
            collective_id=0, has_side_effects=True, vmem_limit_bytes=60 * 1024 * 1024
        ),
        cost_estimate=pl.CostEstimate(flops=3_000_000_000, bytes_accessed=10_000_000, transcendentals=0),
        name="substitution",
    )(child, rhs, link, root, root_rhs[:, 0], structure)
    child_x = child_x.reshape(2, 256, 256).astype(F32)
    return child_x[None, :, None], root_x.astype(F32)[:, None]


def solution(mesh):
    placed = (
        P("leaf", None, "col", None, None),
        P("leaf", None, "row", None, None, "col", None),
        P(None, "row", None, None, "col", None),
        P("leaf", None, "row", None, None, "col", None),
        P(None, "col", None, None),
        P("leaf", None),
    )
    return jax.shard_map(
        on_device,
        mesh=mesh,
        in_specs=placed,
        out_specs=(P("leaf", None, "col", None, None), P(None, "col", None, None)),
        check_vma=False,
    )
```
